32 devices in a mesh: dp: 2 (over core), row: 4 (over y, x), col: 4 (over z).
Axes of the slice: x: 2, y: 2, z: 4, core: 2. Of those that a mesh axis runs over, the one named last changes fastest.
Arguments:
- patches: bfloat16 [1536, 6144], P(('dp', 'col'), 'row'), may hold values from -250 to 250
- norm_gain: float32 [6144], P('row'), may hold values from 0.1 to 1.9
- w_in: bfloat16 [6144, 12288], P('row', 'col'), may hold values from -0.078125 to 0.078125
- w_out: bfloat16 [12288, 6144], P('col', 'row'), may hold values from -0.0546875 to 0.0546875
- out_grad: bfloat16 [1536, 6144], P(('dp', 'col'), 'row'), may hold values from -3 to 3
Outputs:
- branch: bfloat16 [1536, 6144], P(('dp', 'col'), 'row')
- grad_patches: bfloat16 [1536, 6144], P(('dp', 'col'), 'row')
- grad_w_in: float32 [6144, 12288], P('row', 'col')
- grad_w_out: float32 [12288, 6144], P('col', 'row')
- grad_gain: float32 [6144], P('row')
The draws below stay inside these ranges and needn't reach their ends.
All inputs are finite; a program needn't handle non-finite values.
Results may differ from the reference program's by a relative error of at most 0.034.
Values may be sent and summed in bfloat16 or wider, within the bound.
A program may use at most 128 MiB of HBM per device.

```python
import jax
import jax.numpy as jnp
from jax import lax

D = 6144
FF_WIN = 12288
TOK_REP = 768
TOKENS = 1536
N_DP = 2
N_ROW = 4
N_COL = 4


def draw_patches(key, part):
    key = jax.random.fold_in(key, 11)
    keys = jax.random.split(key, 3)
    columns = 3.0 ** (jnp.arange(D, dtype=jnp.float32) / D)
    columns = columns * jnp.exp(jax.random.uniform(keys[1], (D,), jnp.float32, -0.7, 0.7))
    rows = jnp.exp(jax.random.uniform(keys[2], (TOKENS, 1), jnp.float32, 0.0, 2.302585))
    base = jnp.clip(jax.random.normal(keys[0], (TOKENS, D), jnp.float32), -4.0, 4.0)
    return (base * rows * columns).astype(jnp.bfloat16)


def level_of(stream_key, extent, cuts, smallest, largest):
    factor_of = 1.0
    for position, parts in cuts:
        draws = jax.random.uniform(jax.random.fold_in(jax.random.fold_in(stream_key, 6), position), (parts,), jnp.float32, smallest / len(cuts), largest / len(cuts))
        factor_of = factor_of * jnp.repeat(jnp.exp(draws), extent[position] // parts).reshape((-1,) + (1,) * (len(extent) - 1 - position))
    return factor_of


def bell_draw(own_key, dims, scale, bound, cuts=(), kind=jnp.bfloat16):
    drawn = scale * jax.random.normal(own_key, dims, jnp.float32)
    if cuts:
        drawn = drawn * level_of(own_key, dims, cuts, -0.22, 0.18)
    return jnp.clip(drawn, -bound, bound).astype(kind)


def setup_inputs(seed: int = 0) -> dict:
    splits = jax.random.split(jax.random.key(seed), 6)
    return {
        "patches": draw_patches(jax.random.fold_in(splits[5], 71), 0),
        "norm_gain": jnp.clip(1.0 + 0.18 * jax.random.normal(splits[1], (D,), jnp.float32), 0.1, 1.9),
        "w_in": bell_draw(splits[2], (D, FF_WIN), D ** -0.5, 0.078125, ((0, 4), (1, 4))),
        "w_out": bell_draw(splits[3], (FF_WIN, D), FF_WIN ** -0.5, 0.0546875, ((0, 4), (1, 4))),
        "out_grad": bell_draw(splits[4], (TOKENS, D), 0.5, 3.0, ((0, 8), (1, 4))),
    }


def normalize(patches):
    values = patches.astype(jnp.float32)
    average = lax.optimization_barrier(jnp.sum(values, axis=1, keepdims=True)) / D
    squares = lax.optimization_barrier(jnp.sum(values * values, axis=1, keepdims=True)) / D
    inverse = lax.rsqrt(squares - average * average + 1e-06)
    return ((values - average) * inverse, inverse)

def blocked_product(left, right, blocks):
    width = left.shape[1] // blocks

    def step(total, index):
        part_left = lax.dynamic_slice_in_dim(left, index * width, width, 1)
        part_right = lax.dynamic_slice_in_dim(right, index * width, width, 0)
        term = jnp.dot(part_left, part_right, preferred_element_type=jnp.float32).astype(jnp.bfloat16)
        term = lax.optimization_barrier(term)
        return (total + term.astype(jnp.float32), None)
    start_total = jnp.zeros((left.shape[0], right.shape[1]), jnp.float32)
    total, _ = lax.scan(step, start_total, jnp.arange(blocks, dtype=jnp.int32))
    return total

def contract_tokens(left, right):
    return lax.dot_general(left, right, (((0,), (0,)), ((), ())), preferred_element_type=jnp.float32)

def replica_grads(left, right):
    total = jnp.zeros((left.shape[1], right.shape[1]), jnp.float32)
    for group in range(N_DP):
        term = contract_tokens(left[group * TOK_REP:(group + 1) * TOK_REP], right[group * TOK_REP:(group + 1) * TOK_REP])
        term = lax.optimization_barrier(term.astype(jnp.bfloat16))
        total = total + term.astype(jnp.float32)
    return total

def reference(patches, norm_gain, w_in, w_out, out_grad):
    centred, inverse = normalize(patches)
    normed = (centred * norm_gain).astype(jnp.bfloat16)
    pre = blocked_product(normed, w_in, N_ROW)
    activation, slope = jax.vjp(jax.nn.gelu, pre)
    hidden = activation.astype(jnp.bfloat16)
    branch = blocked_product(hidden, w_out, N_COL).astype(jnp.bfloat16)
    hid_grad = blocked_product(out_grad, w_out.T, N_ROW)
    pre_grad = slope(hid_grad)[0].astype(jnp.bfloat16)
    normed_grad = blocked_product(pre_grad, w_in.T, N_COL)
    grad_w_in = replica_grads(normed, pre_grad)
    grad_w_out = replica_grads(hidden, out_grad)
    grad_gain = lax.optimization_barrier(jnp.sum(normed_grad * centred, axis=0))
    scaled = normed_grad * norm_gain
    first = lax.optimization_barrier(jnp.sum(scaled, axis=1, keepdims=True)) / D
    second = lax.optimization_barrier(jnp.sum(scaled * centred, axis=1, keepdims=True)) / D
    grad_patches = (inverse * (scaled - first - centred * second)).astype(jnp.bfloat16)
    return (branch, grad_patches, grad_w_in, grad_w_out, grad_gain)
```

```python
import functools

import jax
import jax.numpy as jnp
from jax import lax
from jax.experimental import pallas as pl
from jax.experimental.pallas import tpu as pltpu
from jax.sharding import PartitionSpec as P

D = 6144
MESH = pl.DeviceIdType.MESH
F32 = jnp.float32
BF16 = jnp.bfloat16

COT, NRM, HG, PRE, HID, PG, BR, NG, ST1, ST2, GG = range(11)


def flip(i, k, n):
    total, bit = 0, 1
    while bit < n:
        k_bit = (k // bit) % 2 if isinstance(k, int) else lax.rem(lax.div(k, jnp.int32(bit)), jnp.int32(2))
        i_bit = lax.rem(lax.div(i, jnp.int32(bit)), jnp.int32(2))
        total = total + lax.rem(i_bit + k_bit, jnp.int32(2)) * bit
        bit *= 2
    return total


def dot(left, right, left_dim=1, right_dim=0):
    return lax.dot_general(left, right, (((left_dim,), (right_dim,)), ((), ())), preferred_element_type=F32)


def gelu_and_slope(x):
    a, b = 0.7978845608028654, 0.044715
    square = x * x
    t = jnp.tanh(a * (x + b * (square * x)))
    half = 0.5 * (1.0 + t)
    return x * half, half + 0.5 * x * (1.0 - t * t) * (a * (1.0 + 3.0 * b * square))


def kernel(
    n, patches, gain, w_in, w_out, out_grad,
    branch, grad_patches, gwi, gwo, ggain,
    wi, wo, cot, nrm, hid, pg, rhg, rpre, stage, rbr, rng, st1, st2, ggr, ggd, lhs, dstage, drecv, obuf,
    wsem, send, recv, dsend, drsem, osem, ggsem, credit,
):
    tb, dl = patches.shape
    fl = w_in.shape[1]
    wf = 256 if fl % 256 == 0 else 128
    wd = 256 if dl % 256 == 0 else 128
    tile = dstage.shape[1]
    r, c, d = lax.axis_index("row"), lax.axis_index("col"), lax.axis_index("dp")

    def rows(j):
        return pl.ds(pl.multiple_of(j * tb, tb), tb)

    def cols(t, width, start=0):
        return pl.ds(pl.multiple_of(start + t * width, width), width)

    load_out = pltpu.make_async_copy(w_out, wo, wsem.at[0])
    load_in = pltpu.make_async_copy(w_in, wi, wsem.at[1])
    load_out.start()
    load_in.start()

    barrier = pltpu.get_barrier_semaphore()
    for k in range(1, n):
        pl.semaphore_signal(barrier, inc=1, device_id={"row": flip(r, k, n)}, device_id_type=MESH)
        pl.semaphore_signal(barrier, inc=1, device_id={"col": flip(c, k, n)}, device_id_type=MESH)
    pl.semaphore_signal(barrier, inc=1, device_id={"dp": 1 - d}, device_id_type=MESH)
    pl.semaphore_wait(barrier, 2 * (n - 1) + 1)

    def copy(kind, src, dst, send_at, recv_at, axis, peer):
        return pltpu.make_async_remote_copy(
            src_ref=src, dst_ref=dst, send_sem=send.at[kind, send_at], recv_sem=recv.at[kind, recv_at],
            device_id={axis: peer}, device_id_type=MESH,
        )

    def cot_copy(k):
        return copy(COT, out_grad, cot.at[rows(c)], k, c, "col", flip(c, k, n))

    def nrm_copy(k):
        return copy(NRM, nrm.at[rows(c)], nrm.at[rows(c)], k, c, "col", flip(c, k, n))

    def hid_copy(k):
        return copy(HID, hid.at[rows(r)], hid.at[rows(r)], k, r, "row", flip(r, k, n))

    def pg_copy(k):
        return copy(PG, pg.at[rows(r)], pg.at[rows(r)], k, r, "row", flip(r, k, n))

    def arrival(kind, ref, source, axis):
        copy(kind, ref, ref, 0, source, axis, source).wait_recv()

    for k in range(1, n):
        cot_copy(k).start()
    cot[rows(c), :] = out_grad[...]

    values = patches[...].astype(F32)
    lane = lax.broadcasted_iota(jnp.int32, (tb, 128), 1)
    st1[r] = jnp.where(
        lane == 0, jnp.sum(values, axis=1, keepdims=True), jnp.sum(values * values, axis=1, keepdims=True)
    )
    for k in range(1, n):
        copy(ST1, st1.at[r], st1.at[r], k, r, "row", flip(r, k, n)).start()

    def hg_copy(kind, dst, j):
        return copy(kind, stage.at[j], dst.at[r], j, r, "row", j)

    def scatter_row(kind, k, panel, product, dst):
        j = flip(c, k, n)
        mine = j == r

        if kind == PRE:
            @pl.when(jnp.logical_not(mine))
            def _():
                hg_copy(HG, rhg, j).wait_send()

        def body(t, carry):
            term = product(panel[rows(j), :], t).astype(BF16)

            @pl.when(mine)
            def _():
                dst[r, :, cols(t, wf)] = term

            @pl.when(jnp.logical_not(mine))
            def _():
                stage[j, :, cols(t, wf)] = term

            return carry

        lax.fori_loop(0, fl // wf, body, 0)

        @pl.when(jnp.logical_not(mine))
        def _():
            hg_copy(kind, dst, j).start()

    def hg_product(left, t):
        return dot(left, wo[cols(t, wf), :], 1, 1)

    def pre_product(left, t):
        return dot(left, wi[:, cols(t, wf)])

    load_out.wait()
    scatter_row(HG, jnp.int32(0), cot, hg_product, rhg)

    for k in range(1, n):
        arrival(ST1, st1.at[flip(r, k, n)], flip(r, k, n), "row")
    sums = st1[0]
    for q in range(1, n):
        sums = sums + st1[q]
    average = sums[:, 0:1] / D
    inverse = lax.rsqrt(sums[:, 1:2] / D - average * average + 1e-06)
    nrm[rows(c), :] = ((patches[...].astype(F32) - average) * inverse * gain[...]).astype(BF16)

    def hg_step(k, carry):
        source = flip(c, k, n)
        arrival(COT, cot.at[rows(source)], source, "col")
        cot_copy(k).wait_send()
        nrm_copy(k).start()
        scatter_row(HG, k, cot, hg_product, rhg)
        return carry

    lax.fori_loop(1, n, hg_step, 0)
    load_in.wait()

    def pre_step(k, carry):
        source = flip(c, k, n)

        @pl.when(k > 0)
        def _():
            arrival(NRM, nrm.at[rows(source)], source, "col")
            nrm_copy(k).wait_send()

        scatter_row(PRE, k, nrm, pre_product, rpre)
        return carry

    lax.fori_loop(0, n, pre_step, 0)

    for k in range(1, n):
        source = flip(r, k, n)
        arrival(HG, rhg.at[source], source, "row")
        arrival(PRE, rpre.at[source], source, "row")

    def hidden_step(t, carry):
        at = cols(t, wf)
        pre, grad = rpre[0, :, at].astype(F32), rhg[0, :, at].astype(F32)
        for q in range(1, n):
            pre = pre + rpre[q, :, at].astype(F32)
            grad = grad + rhg[q, :, at].astype(F32)
        activation, slope = gelu_and_slope(pre)
        hid[rows(r), at] = activation.astype(BF16)
        pg[rows(r), at] = (grad * slope).astype(BF16)
        return carry

    lax.fori_loop(0, fl // wf, hidden_step, 0)
    for k in range(1, n):
        hid_copy(k).start()
    for k in range(1, n):
        hg_copy(PRE, rpre, flip(r, k, n)).wait_send()

    def br_copy(kind, dst, j, start):
        return copy(kind, stage.at[j, :, pl.ds(start, dl)], dst.at[c], j, c, "col", j)

    def scatter_col(kind, k, panel, product, dst, start):
        j = flip(r, k, n)
        mine = j == c

        def body(t, carry):
            term = product(panel[rows(j), :], t).astype(BF16)

            @pl.when(mine)
            def _():
                dst[c, :, cols(t, wd)] = term

            @pl.when(jnp.logical_not(mine))
            def _():
                stage[j, :, cols(t, wd, start)] = term

            return carry

        lax.fori_loop(0, dl // wd, body, 0)

        @pl.when(jnp.logical_not(mine))
        def _():
            br_copy(kind, dst, j, start).start()

    def branch_step(k, carry):
        source = flip(r, k, n)

        @pl.when(k > 0)
        def _():
            arrival(HID, hid.at[rows(source)], source, "row")
            hid_copy(k).wait_send()
            pg_copy(k).start()

        scatter_col(BR, k, hid, lambda left, t: dot(left, wo[:, cols(t, wd)]), rbr, 0)
        return carry

    lax.fori_loop(0, n, branch_step, 0)

    def tile_copy(slot):
        return pltpu.make_async_remote_copy(
            src_ref=dstage.at[slot], dst_ref=drecv.at[slot], send_sem=dsend.at[slot], recv_sem=drsem.at[slot],
            device_id={"dp": 1 - d}, device_id_type=MESH,
        )

    def weight_grad(left, right, out, per_row, first, last):
        count = (out.shape[0] // tile) * per_row

        def place(t):
            if per_row == 1:
                return out.at[cols(t, tile), :]
            return out.at[cols(lax.div(t, jnp.int32(per_row)), tile), cols(lax.rem(t, jnp.int32(per_row)), dl)]

        def result_copy(t):
            slot = lax.rem(t, jnp.int32(2))
            return pltpu.make_async_copy(obuf.at[slot], place(t), osem.at[slot])

        def finish(t):
            slot = lax.rem(t, jnp.int32(2))
            tile_copy(slot).wait_send()
            tile_copy(slot).wait_recv()

            @pl.when(t >= 2)
            def _():
                result_copy(t - 2).wait()

            obuf[slot] = (dstage[slot].astype(F32) + drecv[slot].astype(F32)).astype(BF16)
            result_copy(t).start()

            def free():
                pl.semaphore_signal(credit, inc=1, device_id={"dp": 1 - d}, device_id_type=MESH)

            if last:
                pl.when(t < count - 2)(free)
            else:
                free()

        def step(t, carry):
            slot = lax.rem(t, jnp.int32(2))
            lhs[...] = left[:, cols(lax.div(t, jnp.int32(per_row)), tile)].T
            shift = lax.rem(t, jnp.int32(per_row)) * dl

            def part(p, inner):
                dstage[slot, :, cols(p, wd)] = dot(
                    lhs[...], right[:, pl.ds(pl.multiple_of(shift + p * wd, wd), wd)]
                ).astype(BF16)
                return inner

            lax.fori_loop(0, dl // wd, part, 0)

            def claim():
                pl.semaphore_wait(credit, 1)

            if first:
                pl.when(t >= 2)(claim)
            else:
                claim()
            tile_copy(slot).start()

            @pl.when(t >= 1)
            def _():
                finish(t - 1)

            return carry

        lax.fori_loop(0, count, step, 0)
        finish(jnp.int32(count - 1))
        result_copy(jnp.int32(count - 2)).wait()
        result_copy(jnp.int32(count - 1)).wait()

    weight_grad(hid, cot, gwo, 1, True, False)

    def ng_step(k, carry):
        source = flip(r, k, n)

        @pl.when(k > 0)
        def _():
            arrival(PG, pg.at[rows(source)], source, "row")
            pg_copy(k).wait_send()

        scatter_col(NG, k, pg, lambda left, t: dot(left, wi[cols(t, wd), :], 1, 1), rng, dl)
        return carry

    lax.fori_loop(0, n, ng_step, 0)
    weight_grad(nrm, pg, gwi, fl // dl, False, True)

    for k in range(1, n):
        arrival(NG, rng.at[flip(c, k, n)], flip(c, k, n), "col")
    total = rng[0].astype(F32)
    for q in range(1, n):
        total = total + rng[q].astype(F32)
    centred = (patches[...].astype(F32) - average) * inverse
    weighted = total * centred
    ggr[c] = jnp.broadcast_to(jnp.sum(weighted, axis=0, keepdims=True), (8, dl))
    scaled = total * gain[...]
    st2[r] = jnp.where(
        lane == 0, jnp.sum(scaled, axis=1, keepdims=True),
        jnp.sum(weighted * gain[...], axis=1, keepdims=True),
    )
    for k in range(1, n):
        copy(ST2, st2.at[r], st2.at[r], k, r, "row", flip(r, k, n)).start()
        copy(GG, ggr.at[c], ggr.at[c], k, c, "col", flip(c, k, n)).start()
    for k in range(1, n):
        arrival(BR, rbr.at[flip(c, k, n)], flip(c, k, n), "col")
    out = rbr[0].astype(F32)
    for q in range(1, n):
        out = out + rbr[q].astype(F32)
    branch[...] = out.astype(BF16)

    for k in range(1, n):
        arrival(GG, ggr.at[flip(c, k, n)], flip(c, k, n), "col")
    own = ggr[0]
    for q in range(1, n):
        own = own + ggr[q]
    ggd[0] = own
    gain_copy = pltpu.make_async_remote_copy(
        src_ref=ggd.at[0], dst_ref=ggd.at[1], send_sem=ggsem.at[0], recv_sem=ggsem.at[1],
        device_id={"dp": 1 - d}, device_id_type=MESH,
    )
    gain_copy.start()
    for k in range(1, n):
        arrival(ST2, st2.at[flip(r, k, n)], flip(r, k, n), "row")
    sums = st2[0]
    for q in range(1, n):
        sums = sums + st2[q]
    first, second = sums[:, 0:1] / D, sums[:, 1:2] / D
    total = rng[0].astype(F32)
    for q in range(1, n):
        total = total + rng[q].astype(F32)
    centred = (patches[...].astype(F32) - average) * inverse
    grad_patches[...] = (inverse * (total * gain[...] - first - centred * second)).astype(BF16)
    gain_copy.wait()
    ggain[...] = ggd[0] + ggd[1]

    for k in range(1, n):
        copy(ST1, st1.at[r], st1.at[r], k, r, "row", flip(r, k, n)).wait_send()
        copy(ST2, st2.at[r], st2.at[r], k, r, "row", flip(r, k, n)).wait_send()
        copy(GG, ggr.at[c], ggr.at[c], k, c, "col", flip(c, k, n)).wait_send()
        br_copy(BR, rbr, flip(c, k, n), 0).wait_send()
        br_copy(NG, rng, flip(c, k, n), dl).wait_send()


def shards(n, patches, norm_gain, w_in, w_out, out_grad):
    tb, dl = patches.shape
    fl = w_in.shape[1]
    tile = 256 if dl % 256 == 0 and fl % 256 == 0 else 128
    vmem = pl.BlockSpec(memory_space=pltpu.VMEM)
    hbm = pl.BlockSpec(memory_space=pl.ANY)
    out = jax.ShapeDtypeStruct
    flops = 12 * n * tb * dl * fl
    branch, grad_patches, gwi, gwo, ggain = pl.pallas_call(
        functools.partial(kernel, n),
        out_shape=(
            out((tb, dl), BF16), out((tb, dl), BF16), out((dl, fl), BF16), out((fl, dl), BF16), out((8, dl), F32),
        ),
        in_specs=[vmem, vmem, hbm, hbm, vmem],
        out_specs=(vmem, vmem, hbm, hbm, vmem),
        scratch_shapes=[
            pltpu.VMEM((dl, fl), BF16),
            pltpu.VMEM((fl, dl), BF16),
            pltpu.VMEM((n * tb, dl), BF16),
            pltpu.VMEM((n * tb, dl), BF16),
            pltpu.VMEM((n * tb, fl), BF16),
            pltpu.VMEM((n * tb, fl), BF16),
            pltpu.VMEM((n, tb, fl), BF16),
            pltpu.VMEM((n, tb, fl), BF16),
            pltpu.VMEM((n, tb, fl), BF16),
            pltpu.VMEM((n, tb, dl), BF16),
            pltpu.VMEM((n, tb, dl), BF16),
            pltpu.VMEM((n, tb, 128), F32),
            pltpu.VMEM((n, tb, 128), F32),
            pltpu.VMEM((n, 8, dl), F32),
            pltpu.VMEM((2, 8, dl), F32),
            pltpu.VMEM((tile, n * tb), BF16),
            pltpu.VMEM((2, tile, dl), BF16),
            pltpu.VMEM((2, tile, dl), BF16),
            pltpu.VMEM((2, tile, dl), BF16),
            pltpu.SemaphoreType.DMA((2,)),
            pltpu.SemaphoreType.DMA((11, n)),
            pltpu.SemaphoreType.DMA((11, n)),
            pltpu.SemaphoreType.DMA((2,)),
            pltpu.SemaphoreType.DMA((2,)),
            pltpu.SemaphoreType.DMA((2,)),
            pltpu.SemaphoreType.DMA((2,)),
            pltpu.SemaphoreType.REGULAR,
        ],
        compiler_params=pltpu.CompilerParams(
            collective_id=0, has_side_effects=True, vmem_limit_bytes=63 * 1024 * 1024
        ),
        cost_estimate=pl.CostEstimate(flops=flops, bytes_accessed=8 * dl * fl, transcendentals=tb * fl),
    )(patches, norm_gain.reshape(1, dl), w_in, w_out, out_grad)
    return branch, grad_patches, gwi.astype(F32), gwo.astype(F32), ggain[0]


def solution(mesh):
    n = mesh.shape["row"]
    if mesh.shape["col"] != n or mesh.shape["dp"] != 2 or n & (n - 1):
        raise ValueError("unsupported mesh")
    return jax.shard_map(
        functools.partial(shards, n),
        mesh=mesh,
        in_specs=(
            P(("dp", "col"), "row"),
            P("row"),
            P("row", "col"),
            P("col", "row"),
            P(("dp", "col"), "row"),
        ),
        out_specs=(
            P(("dp", "col"), "row"),
            P(("dp", "col"), "row"),
            P("row", "col"),
            P("col", "row"),
            P("row"),
        ),
        check_vma=False,
    )
```

```python
import functools

import jax
import jax.numpy as jnp
from jax import lax
from jax.experimental import pallas as pl
from jax.experimental.pallas import tpu as pltpu
from jax.sharding import PartitionSpec as P

D = 6144
MESH = pl.DeviceIdType.MESH
F32 = jnp.float32
BF16 = jnp.bfloat16

COT, NRM, HG, PRE, HID, PG, BR, NG, ST1, ST2, GG = range(11)


def flip(i, k, n):
    total, bit = 0, 1
    while bit < n:
        k_bit = (k // bit) % 2 if isinstance(k, int) else lax.rem(lax.div(k, jnp.int32(bit)), jnp.int32(2))
        i_bit = lax.rem(lax.div(i, jnp.int32(bit)), jnp.int32(2))
        total = total + lax.rem(i_bit + k_bit, jnp.int32(2)) * bit
        bit *= 2
    return total


def dot(left, right, left_dim=1, right_dim=0):
    return lax.dot_general(left, right, (((left_dim,), (right_dim,)), ((), ())), preferred_element_type=F32)


def gelu_and_slope(x):
    a, b = 0.7978845608028654, 0.044715
    square = x * x
    t = jnp.tanh(a * (x + b * (square * x)))
    half = 0.5 * (1.0 + t)
    return x * half, half + 0.5 * x * (1.0 - t * t) * (a * (1.0 + 3.0 * b * square))


def weight_grads(tile, wd, dl, d, lhs, dstage, drecv, dsend, drsem, osem, credit):
    def cols(t, width, start=0):
        return pl.ds(pl.multiple_of(start + t * width, width), width)

    def tile_copy(slot):
        return pltpu.make_async_remote_copy(
            src_ref=dstage.at[slot], dst_ref=drecv.at[slot], send_sem=dsend.at[slot], recv_sem=drsem.at[slot],
            device_id={"dp": 1 - d}, device_id_type=MESH,
        )

    def weight_grad(left, right, out, per_row, first, last):
        count = (out.shape[0] // tile) * per_row

        def place(t):
            if per_row == 1:
                return out.at[cols(t, tile), :]
            return out.at[cols(lax.div(t, jnp.int32(per_row)), tile), cols(lax.rem(t, jnp.int32(per_row)), dl)]

        def result_copy(t):
            slot = lax.rem(t, jnp.int32(2))
            return pltpu.make_async_copy(drecv.at[slot], place(t), osem.at[slot])

        def finish(t):
            slot = lax.rem(t, jnp.int32(2))
            tile_copy(slot).wait_send()
            tile_copy(slot).wait_recv()
            drecv[slot] = (dstage[slot].astype(F32) + drecv[slot].astype(F32)).astype(BF16)
            result_copy(t).start()

        def retire(t):
            result_copy(t).wait()

            def free():
                pl.semaphore_signal(credit, inc=1, device_id={"dp": 1 - d}, device_id_type=MESH)

            if last:
                pl.when(t < count - 2)(free)
            else:
                free()

        def step(t, carry):
            slot = lax.rem(t, jnp.int32(2))
            lhs[...] = left[:, cols(lax.div(t, jnp.int32(per_row)), tile)].T
            shift = lax.rem(t, jnp.int32(per_row)) * dl

            def part(p, inner):
                dstage[slot, :, cols(p, wd)] = dot(
                    lhs[...], right[:, pl.ds(pl.multiple_of(shift + p * wd, wd), wd)]
                ).astype(BF16)
                return inner

            lax.fori_loop(0, dl // wd, part, 0)

            @pl.when(t >= 2)
            def _():
                retire(t - 2)

            def claim():
                pl.semaphore_wait(credit, 1)

            if first:
                pl.when(t >= 2)(claim)
            else:
                claim()
            tile_copy(slot).start()

            @pl.when(t >= 1)
            def _():
                finish(t - 1)

            return carry

        lax.fori_loop(0, count, step, 0)
        finish(jnp.int32(count - 1))
        retire(jnp.int32(count - 2))
        retire(jnp.int32(count - 1))

    return weight_grad


def kernel_split(
    n, patches, gain, w_in, w_out, out_grad,
    branch, grad_patches, gwi, gwo, ggain,
    wi, wo, cot, nrm, hid, pg, rhg, rpre, stage, stage2, rbr, rng, st1, st2, ggr, ggd, lhs, dstage, drecv,
    wsem, send, recv, dsend, drsem, osem, ggsem, credit,
):
    tb, dl = patches.shape
    fl = w_in.shape[1]
    sb = tb // n
    wf = 256 if fl % 256 == 0 else 128
    wd = 256 if dl % 256 == 0 else 128
    tile = dstage.shape[1]
    r, c, d = lax.axis_index("row"), lax.axis_index("col"), lax.axis_index("dp")
    weight_grad = weight_grads(tile, wd, dl, d, lhs, dstage, drecv, dsend, drsem, osem, credit)

    def rows(j):
        return pl.ds(pl.multiple_of(j * tb, tb), tb)

    def piece(j, q):
        return pl.ds(pl.multiple_of(j * tb + q * sb, sb), sb)

    def part(q):
        return pl.ds(pl.multiple_of(q * sb, sb), sb)

    def cols(t, width, start=0):
        return pl.ds(pl.multiple_of(start + t * width, width), width)

    load_out = pltpu.make_async_copy(w_out, wo, wsem.at[0])
    load_in = pltpu.make_async_copy(w_in, wi, wsem.at[1])
    load_out.start()
    load_in.start()

    barrier = pltpu.get_barrier_semaphore()
    for k in range(1, n):
        pl.semaphore_signal(barrier, inc=1, device_id={"row": flip(r, k, n)}, device_id_type=MESH)
        pl.semaphore_signal(barrier, inc=1, device_id={"col": flip(c, k, n)}, device_id_type=MESH)
    pl.semaphore_signal(barrier, inc=1, device_id={"dp": 1 - d}, device_id_type=MESH)
    pl.semaphore_wait(barrier, 2 * (n - 1) + 1)

    def copy(kind, src, dst, at, axis, peer):
        return pltpu.make_async_remote_copy(
            src_ref=src, dst_ref=dst, send_sem=send.at[kind, at], recv_sem=recv.at[kind, at],
            device_id={axis: peer}, device_id_type=MESH,
        )

    def cot_copy(k):
        return copy(COT, out_grad, cot.at[rows(c)], k, "col", flip(c, k, n))

    def nrm_copy(k):
        return copy(NRM, nrm.at[rows(c)], nrm.at[rows(c)], k, "col", flip(c, k, n))

    def st1_copy(m):
        return copy(ST1, st1.at[0], st1.at[m], m, "row", flip(r, m, n))

    def st2_copy(m):
        return copy(ST2, st2.at[0], st2.at[m], m, "row", flip(r, m, n))

    def gg_copy(k):
        return copy(GG, ggr.at[0], ggr.at[k], k, "col", flip(c, k, n))

    def scatter_copy(kind, src, dst, j, m):
        peer = flip(r, m, n)
        return copy(kind, src.at[j, part(peer)], dst.at[m - 1, part(j)], j * n + m, "row", peer)

    def gather_copy(kind, panel, j, m):
        return copy(kind, panel.at[piece(j, r)], panel.at[piece(j, r)], j * n + m, "row", flip(r, m, n))

    def back_copy(kind, dst, k, start):
        j = flip(c, k, n)
        return copy(kind, stage.at[j, :, pl.ds(start, dl)], dst.at[k - 1], k, "col", j)

    cot_copy(1).start()
    if n > 2:
        cot_copy(2).start()
    own_cot = pltpu.make_async_copy(out_grad, cot.at[rows(c)], wsem.at[2])
    own_cot.start()

    values = patches[...].astype(F32)
    lane = lax.broadcasted_iota(jnp.int32, (tb, 128), 1)
    st1[0] = jnp.where(
        lane == 0, jnp.sum(values, axis=1, keepdims=True), jnp.sum(values * values, axis=1, keepdims=True)
    )
    for m in range(1, n):
        st1_copy(m).start()

    def hid_grad_terms(j):
        def body(t, carry):
            stage[j, :, cols(t, wf)] = dot(cot[rows(j), :], wo[cols(t, wf), :], 1, 1).astype(BF16)
            return carry

        lax.fori_loop(0, fl // wf, body, 0)
        for m in range(1, n):
            scatter_copy(HG, stage, rhg, j, m).start()

    def pre_terms(j):
        def body(t, carry):
            stage2[j, :, cols(t, wf)] = dot(nrm[rows(j), :], wi[:, cols(t, wf)]).astype(BF16)
            return carry

        lax.fori_loop(0, fl // wf, body, 0)
        for m in range(1, n):
            scatter_copy(PRE, stage2, rpre, j, m).start()

    def hidden(j):
        for m in range(1, n):
            scatter_copy(HG, stage, rhg, j, m).wait_recv()
            scatter_copy(PRE, stage2, rpre, j, m).wait_recv()

        def body(t, carry):
            at = cols(t, wf)
            pre, grad = stage2[j, part(r), at].astype(F32), stage[j, part(r), at].astype(F32)
            for m in range(1, n):
                pre = pre + rpre[m - 1, part(j), at].astype(F32)
                grad = grad + rhg[m - 1, part(j), at].astype(F32)
            activation, slope = gelu_and_slope(pre)
            hid[piece(j, r), at] = activation.astype(BF16)
            pg[piece(j, r), at] = (grad * slope).astype(BF16)
            return carry

        lax.fori_loop(0, fl // wf, body, 0)
        for m in range(1, n):
            gather_copy(HID, hid, j, m).start()
        for m in range(1, n):
            gather_copy(PG, pg, j, m).start()

    def back(k):
        j = flip(c, k, n)
        for m in range(1, n):
            scatter_copy(HG, stage, rhg, j, m).wait_send()
        for m in range(1, n):
            gather_copy(HID, hid, j, m).wait_recv()

        def branch_body(t, carry):
            stage[j, :, cols(t, wd)] = dot(hid[rows(j), :], wo[:, cols(t, wd)]).astype(BF16)
            return carry

        lax.fori_loop(0, dl // wd, branch_body, 0)
        if k > 0:
            back_copy(BR, rbr, k, 0).start()
        for m in range(1, n):
            gather_copy(PG, pg, j, m).wait_recv()

        def grad_body(t, carry):
            stage[j, :, cols(t, wd, dl)] = dot(pg[rows(j), :], wi[cols(t, wd), :], 1, 1).astype(BF16)
            return carry

        lax.fori_loop(0, dl // wd, grad_body, 0)
        if k > 0:
            back_copy(NG, rng, k, dl).start()

    own_cot.wait()
    load_out.wait()
    hid_grad_terms(c)

    sums = st1[0]
    for m in range(1, n):
        st1_copy(m).wait_recv()
        sums = sums + st1[m]
    average = sums[:, 0:1] / D
    inverse = lax.rsqrt(sums[:, 1:2] / D - average * average + 1e-06)
    nrm[rows(c), :] = ((patches[...].astype(F32) - average) * inverse * gain[...]).astype(BF16)
    nrm_copy(1).start()
    if n > 2:
        nrm_copy(2).start()
    load_in.wait()
    pre_terms(c)

    for k in range(1, n):
        cot_copy(k).wait_recv()
        if k + 2 < n:
            cot_copy(k).wait_send()
            cot_copy(k + 2).start()
        hid_grad_terms(flip(c, k, n))
        nrm_copy(k).wait_recv()
        if k + 2 < n:
            nrm_copy(k).wait_send()
            nrm_copy(k + 2).start()
        pre_terms(flip(c, k, n))
        hidden(flip(c, k - 1, n))
        if k > 1:
            back(k - 2)
    hidden(flip(c, n - 1, n))
    for k in range(max(n - 2, 0), n):
        back(k)

    weight_grad(hid, cot, gwo, 1, True, False)

    def sum_back(dst, start):
        total = stage[c, :, pl.ds(start, dl)].astype(F32)
        for k in range(1, n):
            total = total + dst[k - 1].astype(F32)
        return total

    for k in range(1, n):
        back_copy(NG, rng, k, dl).wait_recv()
    total = sum_back(rng, dl)
    weighted = total * ((patches[...].astype(F32) - average) * inverse)
    ggr[0] = jnp.broadcast_to(jnp.sum(weighted, axis=0, keepdims=True), (8, dl))
    st2[0] = jnp.where(
        lane == 0, jnp.sum(total * gain[...], axis=1, keepdims=True),
        jnp.sum(weighted * gain[...], axis=1, keepdims=True),
    )
    for m in range(1, n):
        st2_copy(m).start()
    for k in range(1, n):
        gg_copy(k).start()
    for k in range(1, n):
        back_copy(BR, rbr, k, 0).wait_recv()
    branch[...] = sum_back(rbr, 0).astype(BF16)
    own = ggr[0]
    for k in range(1, n):
        gg_copy(k).wait_recv()
        own = own + ggr[k]
    ggd[0] = own
    gain_copy = pltpu.make_async_remote_copy(
        src_ref=ggd.at[0], dst_ref=ggd.at[1], send_sem=ggsem.at[0], recv_sem=ggsem.at[1],
        device_id={"dp": 1 - d}, device_id_type=MESH,
    )
    gain_copy.start()

    weight_grad(nrm, pg, gwi, fl // dl, False, True)

    sums = st2[0]
    for m in range(1, n):
        st2_copy(m).wait_recv()
        sums = sums + st2[m]
    first, second = sums[:, 0:1] / D, sums[:, 1:2] / D
    centred = (patches[...].astype(F32) - average) * inverse
    grad_patches[...] = (inverse * (sum_back(rng, dl) * gain[...] - first - centred * second)).astype(BF16)
    gain_copy.wait()
    ggain[...] = ggd[0] + ggd[1]

    for m in range(1, n):
        st1_copy(m).wait_send()
        st2_copy(m).wait_send()
        gg_copy(m).wait_send()
        back_copy(BR, rbr, m, 0).wait_send()
        back_copy(NG, rng, m, dl).wait_send()
        if m + 2 >= n:
            cot_copy(m).wait_send()
            nrm_copy(m).wait_send()
        for k in range(n):
            j = flip(c, k, n)
            scatter_copy(PRE, stage2, rpre, j, m).wait_send()
            gather_copy(HID, hid, j, m).wait_send()
            gather_copy(PG, pg, j, m).wait_send()


def kernel(
    n, patches, gain, w_in, w_out, out_grad,
    branch, grad_patches, gwi, gwo, ggain,
    wi, wo, cot, nrm, hid, pg, rhg, rpre, stage, rbr, rng, st1, st2, ggr, ggd, lhs, dstage, drecv,
    wsem, send, recv, dsend, drsem, osem, ggsem, credit,
):
    tb, dl = patches.shape
    fl = w_in.shape[1]
    wf = 256 if fl % 256 == 0 else 128
    wd = 256 if dl % 256 == 0 else 128
    tile = dstage.shape[1]
    r, c, d = lax.axis_index("row"), lax.axis_index("col"), lax.axis_index("dp")

    def rows(j):
        return pl.ds(pl.multiple_of(j * tb, tb), tb)

    def cols(t, width, start=0):
        return pl.ds(pl.multiple_of(start + t * width, width), width)

    load_out = pltpu.make_async_copy(w_out, wo, wsem.at[0])
    load_in = pltpu.make_async_copy(w_in, wi, wsem.at[1])
    load_out.start()
    load_in.start()

    barrier = pltpu.get_barrier_semaphore()
    for k in range(1, n):
        pl.semaphore_signal(barrier, inc=1, device_id={"row": flip(r, k, n)}, device_id_type=MESH)
        pl.semaphore_signal(barrier, inc=1, device_id={"col": flip(c, k, n)}, device_id_type=MESH)
    pl.semaphore_signal(barrier, inc=1, device_id={"dp": 1 - d}, device_id_type=MESH)
    pl.semaphore_wait(barrier, 2 * (n - 1) + 1)

    def copy(kind, src, dst, send_at, recv_at, axis, peer):
        return pltpu.make_async_remote_copy(
            src_ref=src, dst_ref=dst, send_sem=send.at[kind, send_at], recv_sem=recv.at[kind, recv_at],
            device_id={axis: peer}, device_id_type=MESH,
        )

    def cot_copy(k):
        return copy(COT, out_grad, cot.at[rows(c)], k, c, "col", flip(c, k, n))

    def nrm_copy(k):
        return copy(NRM, nrm.at[rows(c)], nrm.at[rows(c)], k, c, "col", flip(c, k, n))

    def hid_copy(k):
        return copy(HID, hid.at[rows(r)], hid.at[rows(r)], k, r, "row", flip(r, k, n))

    def pg_copy(k):
        return copy(PG, pg.at[rows(r)], pg.at[rows(r)], k, r, "row", flip(r, k, n))

    def arrival(kind, ref, source, axis):
        copy(kind, ref, ref, 0, source, axis, source).wait_recv()

    for k in range(1, n):
        cot_copy(k).start()
    own_cot = pltpu.make_async_copy(out_grad, cot.at[rows(c)], wsem.at[2])
    own_cot.start()

    values = patches[...].astype(F32)
    lane = lax.broadcasted_iota(jnp.int32, (tb, 128), 1)
    st1[r] = jnp.where(
        lane == 0, jnp.sum(values, axis=1, keepdims=True), jnp.sum(values * values, axis=1, keepdims=True)
    )
    for k in range(1, n):
        copy(ST1, st1.at[r], st1.at[r], k, r, "row", flip(r, k, n)).start()

    def hg_copy(kind, dst, j):
        return copy(kind, stage.at[j], dst.at[r], j, r, "row", j)

    def scatter_row(kind, k, panel, product, dst):
        j = flip(c, k, n)
        mine = j == r

        if kind == PRE:
            @pl.when(jnp.logical_not(mine))
            def _():
                hg_copy(HG, rhg, j).wait_send()

        def body(t, carry):
            term = product(panel[rows(j), :], t).astype(BF16)

            @pl.when(mine)
            def _():
                dst[r, :, cols(t, wf)] = term

            @pl.when(jnp.logical_not(mine))
            def _():
                stage[j, :, cols(t, wf)] = term

            return carry

        lax.fori_loop(0, fl // wf, body, 0)

        @pl.when(jnp.logical_not(mine))
        def _():
            hg_copy(kind, dst, j).start()

    def hg_product(left, t):
        return dot(left, wo[cols(t, wf), :], 1, 1)

    def pre_product(left, t):
        return dot(left, wi[:, cols(t, wf)])

    own_cot.wait()
    load_out.wait()
    scatter_row(HG, jnp.int32(0), cot, hg_product, rhg)

    for k in range(1, n):
        arrival(ST1, st1.at[flip(r, k, n)], flip(r, k, n), "row")
    sums = st1[0]
    for q in range(1, n):
        sums = sums + st1[q]
    average = sums[:, 0:1] / D
    inverse = lax.rsqrt(sums[:, 1:2] / D - average * average + 1e-06)
    nrm[rows(c), :] = ((patches[...].astype(F32) - average) * inverse * gain[...]).astype(BF16)

    def hg_step(k, carry):
        source = flip(c, k, n)
        arrival(COT, cot.at[rows(source)], source, "col")
        cot_copy(k).wait_send()
        nrm_copy(k).start()
        scatter_row(HG, k, cot, hg_product, rhg)
        return carry

    lax.fori_loop(1, n, hg_step, 0)
    load_in.wait()

    def pre_step(k, carry):
        source = flip(c, k, n)

        @pl.when(k > 0)
        def _():
            arrival(NRM, nrm.at[rows(source)], source, "col")
            nrm_copy(k).wait_send()

        scatter_row(PRE, k, nrm, pre_product, rpre)
        return carry

    lax.fori_loop(0, n, pre_step, 0)

    for k in range(1, n):
        source = flip(r, k, n)
        arrival(HG, rhg.at[source], source, "row")
        arrival(PRE, rpre.at[source], source, "row")

    def hidden_step(t, carry):
        at = cols(t, wf)
        pre, grad = rpre[0, :, at].astype(F32), rhg[0, :, at].astype(F32)
        for q in range(1, n):
            pre = pre + rpre[q, :, at].astype(F32)
            grad = grad + rhg[q, :, at].astype(F32)
        activation, slope = gelu_and_slope(pre)
        hid[rows(r), at] = activation.astype(BF16)
        pg[rows(r), at] = (grad * slope).astype(BF16)
        return carry

    lax.fori_loop(0, fl // wf, hidden_step, 0)
    for k in range(1, n):
        hid_copy(k).start()
    for k in range(1, n):
        hg_copy(PRE, rpre, flip(r, k, n)).wait_send()

    def br_copy(kind, dst, j, start):
        return copy(kind, stage.at[j, :, pl.ds(start, dl)], dst.at[c], j, c, "col", j)

    def scatter_col(kind, k, panel, product, dst, start):
        j = flip(r, k, n)
        mine = j == c

        def body(t, carry):
            term = product(panel[rows(j), :], t).astype(BF16)

            @pl.when(mine)
            def _():
                dst[c, :, cols(t, wd)] = term

            @pl.when(jnp.logical_not(mine))
            def _():
                stage[j, :, cols(t, wd, start)] = term

            return carry

        lax.fori_loop(0, dl // wd, body, 0)

        @pl.when(jnp.logical_not(mine))
        def _():
            br_copy(kind, dst, j, start).start()

    def branch_step(k, carry):
        source = flip(r, k, n)

        @pl.when(k > 0)
        def _():
            arrival(HID, hid.at[rows(source)], source, "row")
            hid_copy(k).wait_send()
            pg_copy(k).start()

        scatter_col(BR, k, hid, lambda left, t: dot(left, wo[:, cols(t, wd)]), rbr, 0)
        return carry

    lax.fori_loop(0, n, branch_step, 0)

    weight_grad = weight_grads(tile, wd, dl, d, lhs, dstage, drecv, dsend, drsem, osem, credit)
    weight_grad(hid, cot, gwo, 1, True, False)

    def ng_step(k, carry):
        source = flip(r, k, n)

        @pl.when(k > 0)
        def _():
            arrival(PG, pg.at[rows(source)], source, "row")
            pg_copy(k).wait_send()

        scatter_col(NG, k, pg, lambda left, t: dot(left, wi[cols(t, wd), :], 1, 1), rng, dl)
        return carry

    lax.fori_loop(0, n, ng_step, 0)
    weight_grad(nrm, pg, gwi, fl // dl, False, True)

    for k in range(1, n):
        arrival(NG, rng.at[flip(c, k, n)], flip(c, k, n), "col")
    total = rng[0].astype(F32)
    for q in range(1, n):
        total = total + rng[q].astype(F32)
    centred = (patches[...].astype(F32) - average) * inverse
    weighted = total * centred
    ggr[c] = jnp.broadcast_to(jnp.sum(weighted, axis=0, keepdims=True), (8, dl))
    scaled = total * gain[...]
    st2[r] = jnp.where(
        lane == 0, jnp.sum(scaled, axis=1, keepdims=True),
        jnp.sum(weighted * gain[...], axis=1, keepdims=True),
    )
    for k in range(1, n):
        copy(ST2, st2.at[r], st2.at[r], k, r, "row", flip(r, k, n)).start()
        copy(GG, ggr.at[c], ggr.at[c], k, c, "col", flip(c, k, n)).start()
    for k in range(1, n):
        arrival(BR, rbr.at[flip(c, k, n)], flip(c, k, n), "col")
    out = rbr[0].astype(F32)
    for q in range(1, n):
        out = out + rbr[q].astype(F32)
    branch[...] = out.astype(BF16)

    for k in range(1, n):
        arrival(GG, ggr.at[flip(c, k, n)], flip(c, k, n), "col")
    own = ggr[0]
    for q in range(1, n):
        own = own + ggr[q]
    ggd[0] = own
    gain_copy = pltpu.make_async_remote_copy(
        src_ref=ggd.at[0], dst_ref=ggd.at[1], send_sem=ggsem.at[0], recv_sem=ggsem.at[1],
        device_id={"dp": 1 - d}, device_id_type=MESH,
    )
    gain_copy.start()
    for k in range(1, n):
        arrival(ST2, st2.at[flip(r, k, n)], flip(r, k, n), "row")
    sums = st2[0]
    for q in range(1, n):
        sums = sums + st2[q]
    first, second = sums[:, 0:1] / D, sums[:, 1:2] / D
    total = rng[0].astype(F32)
    for q in range(1, n):
        total = total + rng[q].astype(F32)
    centred = (patches[...].astype(F32) - average) * inverse
    grad_patches[...] = (inverse * (total * gain[...] - first - centred * second)).astype(BF16)
    gain_copy.wait()
    ggain[...] = ggd[0] + ggd[1]

    for k in range(1, n):
        copy(ST1, st1.at[r], st1.at[r], k, r, "row", flip(r, k, n)).wait_send()
        copy(ST2, st2.at[r], st2.at[r], k, r, "row", flip(r, k, n)).wait_send()
        copy(GG, ggr.at[c], ggr.at[c], k, c, "col", flip(c, k, n)).wait_send()
        br_copy(BR, rbr, flip(c, k, n), 0).wait_send()
        br_copy(NG, rng, flip(c, k, n), dl).wait_send()


def shards(n, patches, norm_gain, w_in, w_out, out_grad):
    tb, dl = patches.shape
    fl = w_in.shape[1]
    tile = 256 if dl % 256 == 0 and fl % 256 == 0 else 128
    vmem = pl.BlockSpec(memory_space=pltpu.VMEM)
    hbm = pl.BlockSpec(memory_space=pl.ANY)
    out = jax.ShapeDtypeStruct
    flops = 12 * n * tb * dl * fl
    split = tb % (16 * n) == 0
    block = pltpu.VMEM((n, tb, fl), BF16)
    if split:
        body = kernel_split
        landing = [pltpu.VMEM((n - 1, tb, fl), BF16)] * 2 + [block] * 2 + [pltpu.VMEM((n - 1, tb, dl), BF16)] * 2
    else:
        body = kernel
        landing = [block] * 3 + [pltpu.VMEM((n, tb, dl), BF16)] * 2
    branch, grad_patches, gwi, gwo, ggain = pl.pallas_call(
        functools.partial(body, n),
        out_shape=(
            out((tb, dl), BF16), out((tb, dl), BF16), out((dl, fl), BF16), out((fl, dl), BF16), out((8, dl), F32),
        ),
        in_specs=[vmem, vmem, hbm, hbm, hbm],
        out_specs=(vmem, vmem, hbm, hbm, vmem),
        scratch_shapes=[
            pltpu.VMEM((dl, fl), BF16),
            pltpu.VMEM((fl, dl), BF16),
            pltpu.VMEM((n * tb, dl), BF16),
            pltpu.VMEM((n * tb, dl), BF16),
            pltpu.VMEM((n * tb, fl), BF16),
            pltpu.VMEM((n * tb, fl), BF16),
            *landing,
            pltpu.VMEM((n, tb, 128), F32),
            pltpu.VMEM((n, tb, 128), F32),
            pltpu.VMEM((n, 8, dl), F32),
            pltpu.VMEM((2, 8, dl), F32),
            pltpu.VMEM((tile, n * tb), BF16),
            pltpu.VMEM((2, tile, dl), BF16),
            pltpu.VMEM((2, tile, dl), BF16),
            pltpu.SemaphoreType.DMA((3,)),
            pltpu.SemaphoreType.DMA((11, n * n if split else n)),
            pltpu.SemaphoreType.DMA((11, n * n if split else n)),
            pltpu.SemaphoreType.DMA((2,)),
            pltpu.SemaphoreType.DMA((2,)),
            pltpu.SemaphoreType.DMA((2,)),
            pltpu.SemaphoreType.DMA((2,)),
            pltpu.SemaphoreType.REGULAR,
        ],
        compiler_params=pltpu.CompilerParams(
            collective_id=0, has_side_effects=True, vmem_limit_bytes=63 * 1024 * 1024
        ),
        cost_estimate=pl.CostEstimate(flops=flops, bytes_accessed=8 * dl * fl, transcendentals=tb * fl),
    )(patches, norm_gain.reshape(1, dl), w_in, w_out, out_grad)
    return branch, grad_patches, gwi.astype(F32), gwo.astype(F32), ggain[0]


def solution(mesh):
    n = mesh.shape["row"]
    if mesh.shape["col"] != n or mesh.shape["dp"] != 2 or n & (n - 1):
        raise ValueError("unsupported mesh")
    return jax.shard_map(
        functools.partial(shards, n),
        mesh=mesh,
        in_specs=(
            P(("dp", "col"), "row"),
            P("row"),
            P("row", "col"),
            P("col", "row"),
            P(("dp", "col"), "row"),
        ),
        out_specs=(
            P(("dp", "col"), "row"),
            P(("dp", "col"), "row"),
            P("row", "col"),
            P("col", "row"),
            P("row"),
        ),
        check_vma=False,
    )
```

```python
import functools

import jax
import jax.numpy as jnp
from jax import lax
from jax.experimental import pallas as pl
from jax.experimental.pallas import tpu as pltpu
from jax.sharding import PartitionSpec as P

D = 6144
MESH = pl.DeviceIdType.MESH
F32 = jnp.float32
BF16 = jnp.bfloat16

COT, NRM, HG, PRE, HID, PG, BR, NG, ST1, ST2, GG = range(11)


def flip(i, k, n):
    total, bit = 0, 1
    while bit < n:
        k_bit = (k // bit) % 2 if isinstance(k, int) else lax.rem(lax.div(k, jnp.int32(bit)), jnp.int32(2))
        i_bit = lax.rem(lax.div(i, jnp.int32(bit)), jnp.int32(2))
        total = total + lax.rem(i_bit + k_bit, jnp.int32(2)) * bit
        bit *= 2
    return total


def dot(left, right, left_dim=1, right_dim=0):
    return lax.dot_general(left, right, (((left_dim,), (right_dim,)), ((), ())), preferred_element_type=F32)


def gelu_and_slope(x):
    a, b = 0.7978845608028654, 0.044715
    square = x * x
    t = jnp.tanh(a * (x + b * (square * x)))
    half = 0.5 * (1.0 + t)
    return x * half, half + 0.5 * x * (1.0 - t * t) * (a * (1.0 + 3.0 * b * square))


def weight_grads(d, lhs, tm, tn, outgoing, incoming, dsend, drsem, osem, credit):
    def cols(t, width, start=0):
        return pl.ds(pl.multiple_of(start + t * width, width), width)

    def tile_copy(slot):
        return pltpu.make_async_remote_copy(
            src_ref=outgoing(slot), dst_ref=incoming(slot), send_sem=dsend.at[slot], recv_sem=drsem.at[slot],
            device_id={"dp": 1 - d}, device_id_type=MESH,
        )

    def weight_grad(left, right, out, first, last):
        per_row = out.shape[1] // tn
        count = (out.shape[0] // tm) * per_row

        def across(t):
            return cols(lax.rem(t, jnp.int32(per_row)), tn)

        def place(t):
            return out.at[cols(lax.div(t, jnp.int32(per_row)), tm), across(t)]

        def result_copy(t):
            slot = lax.rem(t, jnp.int32(2))
            return pltpu.make_async_copy(incoming(slot), place(t), osem.at[slot])

        def finish(t):
            slot = lax.rem(t, jnp.int32(2))
            tile_copy(slot).wait_send()
            tile_copy(slot).wait_recv()
            total = outgoing(slot)[...].astype(F32) + incoming(slot)[...].astype(F32)
            incoming(slot)[...] = total.astype(BF16)
            result_copy(t).start()

        def retire(t):
            result_copy(t).wait()

            def free():
                pl.semaphore_signal(credit, inc=1, device_id={"dp": 1 - d}, device_id_type=MESH)

            if last:
                pl.when(t < count - 2)(free)
            else:
                free()

        def step(t, carry):
            slot = lax.rem(t, jnp.int32(2))

            @pl.when(lax.rem(t, jnp.int32(per_row)) == 0)
            def _():
                lhs[...] = left[:, cols(lax.div(t, jnp.int32(per_row)), tm)].T

            outgoing(slot)[...] = dot(lhs[...], right[:, across(t)]).astype(BF16)

            @pl.when(t >= 2)
            def _():
                retire(t - 2)

            def claim():
                pl.semaphore_wait(credit, 1)

            if first:
                pl.when(t >= 2)(claim)
            else:
                claim()
            tile_copy(slot).start()

            @pl.when(t >= 1)
            def _():
                finish(t - 1)

            return carry

        lax.fori_loop(0, count, step, 0)
        finish(jnp.int32(count - 1))
        retire(jnp.int32(count - 2))
        retire(jnp.int32(count - 1))

    return weight_grad


def kernel_split(
    n, patches, gain, w_in, w_out, out_grad,
    branch, grad_patches, gwi, gwo, ggain,
    wi, wo, cot, nrm, hid, pg, rhg, rpre, stage, stage2, rbr, rng, st1, st2, ggr, ggd, lhs,
    wsem, send, recv, dsend, drsem, osem, ggsem, credit,
):
    tb, dl = patches.shape
    fl = w_in.shape[1]
    sb = tb // n
    wf = wd = dl // 2
    wg = 256
    r, c, d = lax.axis_index("row"), lax.axis_index("col"), lax.axis_index("dp")
    def rows(j):
        return pl.ds(pl.multiple_of(j * tb, tb), tb)

    def piece(j, q):
        return pl.ds(pl.multiple_of(j * tb + q * sb, sb), sb)

    def part(q):
        return pl.ds(pl.multiple_of(q * sb, sb), sb)

    def cols(t, width, start=0):
        return pl.ds(pl.multiple_of(start + t * width, width), width)

    tm, tn = lhs.shape[0], fl // 4

    weight_grad = weight_grads(
        d, lhs, tm, tn, lambda slot: stage2.at[pl.ds(0, tm), cols(slot, tn)],
        lambda slot: stage2.at[pl.ds(0, tm), cols(slot + 2, tn)], dsend, drsem, osem, credit,
    )

    load_out = pltpu.make_async_copy(w_out, wo, wsem.at[0])
    load_in = pltpu.make_async_copy(w_in, wi, wsem.at[1])
    load_out.start()
    load_in.start()

    barrier = pltpu.get_barrier_semaphore()
    for k in range(1, n):
        pl.semaphore_signal(barrier, inc=1, device_id={"row": flip(r, k, n)}, device_id_type=MESH)
        pl.semaphore_signal(barrier, inc=1, device_id={"col": flip(c, k, n)}, device_id_type=MESH)
    pl.semaphore_signal(barrier, inc=1, device_id={"dp": 1 - d}, device_id_type=MESH)
    pl.semaphore_wait(barrier, 2 * (n - 1) + 1)

    def copy(kind, src, dst, at, axis, peer):
        return pltpu.make_async_remote_copy(
            src_ref=src, dst_ref=dst, send_sem=send.at[kind, at], recv_sem=recv.at[kind, at],
            device_id={axis: peer}, device_id_type=MESH,
        )

    def cot_copy(k):
        return copy(COT, out_grad, cot.at[rows(c)], k, "col", flip(c, k, n))

    def nrm_copy(k):
        return copy(NRM, nrm.at[rows(c)], nrm.at[rows(c)], k, "col", flip(c, k, n))

    def st1_copy(m):
        return copy(ST1, st1.at[0], st1.at[m], m, "row", flip(r, m, n))

    def st2_copy(m):
        return copy(ST2, st2.at[0], st2.at[m], m, "row", flip(r, m, n))

    def gg_copy(k):
        return copy(GG, ggr.at[0], ggr.at[k], k, "col", flip(c, k, n))

    def scatter_copy(kind, src, dst, j, m):
        peer = flip(r, m, n)
        mine = src.at[piece(j, peer)] if kind == PRE else src.at[j, part(peer)]
        return copy(kind, mine, dst.at[m - 1, part(j)], j * n + m, "row", peer)

    def gather_copy(kind, panel, j, m):
        return copy(kind, panel.at[piece(j, r)], panel.at[piece(j, r)], j * n + m, "row", flip(r, m, n))

    def back_copy(kind, dst, k, start):
        j = flip(c, k, n)
        return copy(kind, stage.at[j, :, pl.ds(start, dl)], dst.at[k - 1], k, "col", j)

    cot_copy(1).start()
    if n > 2:
        cot_copy(2).start()
    own_cot = pltpu.make_async_copy(out_grad, cot.at[rows(c)], wsem.at[2])
    own_cot.start()

    values = patches[...].astype(F32)
    lane = lax.broadcasted_iota(jnp.int32, (tb, 128), 1)
    st1[0] = jnp.where(
        lane == 0, jnp.sum(values, axis=1, keepdims=True), jnp.sum(values * values, axis=1, keepdims=True)
    )
    for m in range(1, n):
        st1_copy(m).start()

    def pair(p):
        return pl.ds(pl.multiple_of(p * 2 * tb, 2 * tb), 2 * tb)

    def store(ref, p, at, term):
        term = term.astype(BF16)
        ref[2 * p, :, at] = term[:tb]
        ref[2 * p + 1, :, at] = term[tb:]

    def hid_grad_terms(p):
        def body(t, carry):
            store(stage, p, cols(t, wf), dot(cot[pair(p), :], wo[cols(t, wf), :], 1, 1))
            return carry

        lax.fori_loop(0, fl // wf, body, 0)
        for j in (2 * p, 2 * p + 1):
            for m in range(1, n):
                scatter_copy(HG, stage, rhg, j, m).start()

    def pre_terms(p):
        def body(t, carry):
            stage2[pair(p), cols(t, wf)] = dot(nrm[pair(p), :], wi[:, cols(t, wf)]).astype(BF16)
            return carry

        lax.fori_loop(0, fl // wf, body, 0)
        for j in (2 * p, 2 * p + 1):
            for m in range(1, n):
                scatter_copy(PRE, stage2, rpre, j, m).start()

    def hidden(j):
        for m in range(1, n):
            scatter_copy(HG, stage, rhg, j, m).wait_recv()
            scatter_copy(PRE, stage2, rpre, j, m).wait_recv()

        def body(t, carry):
            at = cols(t, wg)
            pre, grad = stage2[piece(j, r), at].astype(F32), stage[j, part(r), at].astype(F32)
            for m in range(1, n):
                pre = pre + rpre[m - 1, part(j), at].astype(F32)
                grad = grad + rhg[m - 1, part(j), at].astype(F32)
            activation, slope = gelu_and_slope(pre)
            hid[piece(j, r), at] = activation.astype(BF16)
            pg[piece(j, r), at] = (grad * slope).astype(BF16)
            return carry

        lax.fori_loop(0, fl // wg, body, 0)
        for m in range(1, n):
            gather_copy(HID, hid, j, m).start()
        for m in range(1, n):
            gather_copy(PG, pg, j, m).start()

    def back_branch(p, ks):
        for j in (2 * p, 2 * p + 1):
            for m in range(1, n):
                scatter_copy(HG, stage, rhg, j, m).wait_send()
                gather_copy(HID, hid, j, m).wait_recv()

        def body(t, carry):
            store(stage, p, cols(t, wd), dot(hid[pair(p), :], wo[:, cols(t, wd)]))
            return carry

        lax.fori_loop(0, dl // wd, body, 0)
        for k in ks:
            if k > 0:
                back_copy(BR, rbr, k, 0).start()

    def back_grad(p, ks):
        for j in (2 * p, 2 * p + 1):
            for m in range(1, n):
                gather_copy(PG, pg, j, m).wait_recv()

        def body(t, carry):
            store(stage, p, cols(t, wd, dl), dot(pg[pair(p), :], wi[cols(t, wd), :], 1, 1))
            return carry

        lax.fori_loop(0, dl // wd, body, 0)
        for k in ks:
            if k > 0:
                back_copy(NG, rng, k, dl).start()

    own_cot.wait()
    load_out.wait()

    sums = st1[0]
    for m in range(1, n):
        st1_copy(m).wait_recv()
        sums = sums + st1[m]
    average = sums[:, 0:1] / D
    inverse = lax.rsqrt(sums[:, 1:2] / D - average * average + 1e-06)
    nrm[rows(c), :] = ((patches[...].astype(F32) - average) * inverse * gain[...]).astype(BF16)
    nrm_copy(1).start()
    if n > 2:
        nrm_copy(2).start()
    load_in.wait()

    near = lax.div(c, jnp.int32(2))
    pairs = [flip(near, h, n // 2) for h in range(n // 2)]

    def arrived(copy_of, h):
        for k in (2 * h, 2 * h + 1):
            if k > 0:
                copy_of(k).wait_recv()
                if k + 2 < n:
                    copy_of(k).wait_send()
                    copy_of(k + 2).start()

    def members(h):
        return 2 * h, 2 * h + 1

    for h in range(n // 2):
        arrived(cot_copy, h)
        hid_grad_terms(pairs[h])
        if h > 0:
            hidden(2 * pairs[h - 1])
            hidden(2 * pairs[h - 1] + 1)
        arrived(nrm_copy, h)
        pre_terms(pairs[h])
        if h > 0:
            back_branch(pairs[h - 1], members(h - 1))
            back_grad(pairs[h - 1], members(h - 1))
    last = n // 2 - 1
    hidden(2 * pairs[last])
    hidden(2 * pairs[last] + 1)
    back_branch(pairs[last], members(last))
    back_grad(pairs[last], members(last))

    for m in range(1, n):
        for k in range(n):
            scatter_copy(PRE, stage2, rpre, flip(c, k, n), m).wait_send()
    pl.semaphore_signal(credit, inc=2, device_id={"dp": 1 - d}, device_id_type=MESH)
    weight_grad(hid, cot, gwo, False, False)

    def sum_back(dst, start):
        total = stage[c, :, pl.ds(start, dl)].astype(F32)
        for k in range(1, n):
            total = total + dst[k - 1].astype(F32)
        return total

    for k in range(1, n):
        back_copy(NG, rng, k, dl).wait_recv()
    total = sum_back(rng, dl)
    weighted = total * ((patches[...].astype(F32) - average) * inverse)
    ggr[0] = jnp.broadcast_to(jnp.sum(weighted, axis=0, keepdims=True), (8, dl))
    st2[0] = jnp.where(
        lane == 0, jnp.sum(total * gain[...], axis=1, keepdims=True),
        jnp.sum(weighted * gain[...], axis=1, keepdims=True),
    )
    for m in range(1, n):
        st2_copy(m).start()
    for k in range(1, n):
        gg_copy(k).start()
    for k in range(1, n):
        back_copy(BR, rbr, k, 0).wait_recv()
    branch[...] = sum_back(rbr, 0).astype(BF16)
    own = ggr[0]
    for k in range(1, n):
        gg_copy(k).wait_recv()
        own = own + ggr[k]
    ggd[0] = own
    gain_copy = pltpu.make_async_remote_copy(
        src_ref=ggd.at[0], dst_ref=ggd.at[1], send_sem=ggsem.at[0], recv_sem=ggsem.at[1],
        device_id={"dp": 1 - d}, device_id_type=MESH,
    )
    gain_copy.start()

    weight_grad(nrm, pg, gwi, False, True)

    sums = st2[0]
    for m in range(1, n):
        st2_copy(m).wait_recv()
        sums = sums + st2[m]
    first, second = sums[:, 0:1] / D, sums[:, 1:2] / D
    centred = (patches[...].astype(F32) - average) * inverse
    grad_patches[...] = (inverse * (sum_back(rng, dl) * gain[...] - first - centred * second)).astype(BF16)
    gain_copy.wait()
    ggain[...] = ggd[0] + ggd[1]

    for m in range(1, n):
        st1_copy(m).wait_send()
        st2_copy(m).wait_send()
        gg_copy(m).wait_send()
        back_copy(BR, rbr, m, 0).wait_send()
        back_copy(NG, rng, m, dl).wait_send()
        if m + 2 >= n:
            cot_copy(m).wait_send()
            nrm_copy(m).wait_send()
        for k in range(n):
            j = flip(c, k, n)
            gather_copy(HID, hid, j, m).wait_send()
            gather_copy(PG, pg, j, m).wait_send()


def kernel(
    n, patches, gain, w_in, w_out, out_grad,
    branch, grad_patches, gwi, gwo, ggain,
    wi, wo, cot, nrm, hid, pg, rhg, rpre, stage, rbr, rng, st1, st2, ggr, ggd, lhs, dstage, drecv,
    wsem, send, recv, dsend, drsem, osem, ggsem, credit,
):
    tb, dl = patches.shape
    fl = w_in.shape[1]
    wf = 256 if fl % 256 == 0 else 128
    wd = 256 if dl % 256 == 0 else 128
    r, c, d = lax.axis_index("row"), lax.axis_index("col"), lax.axis_index("dp")

    def rows(j):
        return pl.ds(pl.multiple_of(j * tb, tb), tb)

    def cols(t, width, start=0):
        return pl.ds(pl.multiple_of(start + t * width, width), width)

    load_out = pltpu.make_async_copy(w_out, wo, wsem.at[0])
    load_in = pltpu.make_async_copy(w_in, wi, wsem.at[1])
    load_out.start()
    load_in.start()

    barrier = pltpu.get_barrier_semaphore()
    for k in range(1, n):
        pl.semaphore_signal(barrier, inc=1, device_id={"row": flip(r, k, n)}, device_id_type=MESH)
        pl.semaphore_signal(barrier, inc=1, device_id={"col": flip(c, k, n)}, device_id_type=MESH)
    pl.semaphore_signal(barrier, inc=1, device_id={"dp": 1 - d}, device_id_type=MESH)
    pl.semaphore_wait(barrier, 2 * (n - 1) + 1)

    def copy(kind, src, dst, send_at, recv_at, axis, peer):
        return pltpu.make_async_remote_copy(
            src_ref=src, dst_ref=dst, send_sem=send.at[kind, send_at], recv_sem=recv.at[kind, recv_at],
            device_id={axis: peer}, device_id_type=MESH,
        )

    def cot_copy(k):
        return copy(COT, out_grad, cot.at[rows(c)], k, c, "col", flip(c, k, n))

    def nrm_copy(k):
        return copy(NRM, nrm.at[rows(c)], nrm.at[rows(c)], k, c, "col", flip(c, k, n))

    def hid_copy(k):
        return copy(HID, hid.at[rows(r)], hid.at[rows(r)], k, r, "row", flip(r, k, n))

    def pg_copy(k):
        return copy(PG, pg.at[rows(r)], pg.at[rows(r)], k, r, "row", flip(r, k, n))

    def arrival(kind, ref, source, axis):
        copy(kind, ref, ref, 0, source, axis, source).wait_recv()

    for k in range(1, n):
        cot_copy(k).start()
    own_cot = pltpu.make_async_copy(out_grad, cot.at[rows(c)], wsem.at[2])
    own_cot.start()

    values = patches[...].astype(F32)
    lane = lax.broadcasted_iota(jnp.int32, (tb, 128), 1)
    st1[r] = jnp.where(
        lane == 0, jnp.sum(values, axis=1, keepdims=True), jnp.sum(values * values, axis=1, keepdims=True)
    )
    for k in range(1, n):
        copy(ST1, st1.at[r], st1.at[r], k, r, "row", flip(r, k, n)).start()

    def hg_copy(kind, dst, j):
        return copy(kind, stage.at[j], dst.at[r], j, r, "row", j)

    def scatter_row(kind, k, panel, product, dst):
        j = flip(c, k, n)
        mine = j == r

        if kind == PRE:
            @pl.when(jnp.logical_not(mine))
            def _():
                hg_copy(HG, rhg, j).wait_send()

        def body(t, carry):
            term = product(panel[rows(j), :], t).astype(BF16)

            @pl.when(mine)
            def _():
                dst[r, :, cols(t, wf)] = term

            @pl.when(jnp.logical_not(mine))
            def _():
                stage[j, :, cols(t, wf)] = term

            return carry

        lax.fori_loop(0, fl // wf, body, 0)

        @pl.when(jnp.logical_not(mine))
        def _():
            hg_copy(kind, dst, j).start()

    def hg_product(left, t):
        return dot(left, wo[cols(t, wf), :], 1, 1)

    def pre_product(left, t):
        return dot(left, wi[:, cols(t, wf)])

    own_cot.wait()
    load_out.wait()
    scatter_row(HG, jnp.int32(0), cot, hg_product, rhg)

    for k in range(1, n):
        arrival(ST1, st1.at[flip(r, k, n)], flip(r, k, n), "row")
    sums = st1[0]
    for q in range(1, n):
        sums = sums + st1[q]
    average = sums[:, 0:1] / D
    inverse = lax.rsqrt(sums[:, 1:2] / D - average * average + 1e-06)
    nrm[rows(c), :] = ((patches[...].astype(F32) - average) * inverse * gain[...]).astype(BF16)

    def hg_step(k, carry):
        source = flip(c, k, n)
        arrival(COT, cot.at[rows(source)], source, "col")
        cot_copy(k).wait_send()
        nrm_copy(k).start()
        scatter_row(HG, k, cot, hg_product, rhg)
        return carry

    lax.fori_loop(1, n, hg_step, 0)
    load_in.wait()

    def pre_step(k, carry):
        source = flip(c, k, n)

        @pl.when(k > 0)
        def _():
            arrival(NRM, nrm.at[rows(source)], source, "col")
            nrm_copy(k).wait_send()

        scatter_row(PRE, k, nrm, pre_product, rpre)
        return carry

    lax.fori_loop(0, n, pre_step, 0)

    for k in range(1, n):
        source = flip(r, k, n)
        arrival(HG, rhg.at[source], source, "row")
        arrival(PRE, rpre.at[source], source, "row")

    def hidden_step(t, carry):
        at = cols(t, wf)
        pre, grad = rpre[0, :, at].astype(F32), rhg[0, :, at].astype(F32)
        for q in range(1, n):
            pre = pre + rpre[q, :, at].astype(F32)
            grad = grad + rhg[q, :, at].astype(F32)
        activation, slope = gelu_and_slope(pre)
        hid[rows(r), at] = activation.astype(BF16)
        pg[rows(r), at] = (grad * slope).astype(BF16)
        return carry

    lax.fori_loop(0, fl // wf, hidden_step, 0)
    for k in range(1, n):
        hid_copy(k).start()
    for k in range(1, n):
        hg_copy(PRE, rpre, flip(r, k, n)).wait_send()

    def br_copy(kind, dst, j, start):
        return copy(kind, stage.at[j, :, pl.ds(start, dl)], dst.at[c], j, c, "col", j)

    def scatter_col(kind, k, panel, product, dst, start):
        j = flip(r, k, n)
        mine = j == c

        def body(t, carry):
            term = product(panel[rows(j), :], t).astype(BF16)

            @pl.when(mine)
            def _():
                dst[c, :, cols(t, wd)] = term

            @pl.when(jnp.logical_not(mine))
            def _():
                stage[j, :, cols(t, wd, start)] = term

            return carry

        lax.fori_loop(0, dl // wd, body, 0)

        @pl.when(jnp.logical_not(mine))
        def _():
            br_copy(kind, dst, j, start).start()

    def branch_step(k, carry):
        source = flip(r, k, n)

        @pl.when(k > 0)
        def _():
            arrival(HID, hid.at[rows(source)], source, "row")
            hid_copy(k).wait_send()
            pg_copy(k).start()

        scatter_col(BR, k, hid, lambda left, t: dot(left, wo[:, cols(t, wd)]), rbr, 0)
        return carry

    lax.fori_loop(0, n, branch_step, 0)

    weight_grad = weight_grads(
        d, lhs, *dstage.shape[1:], lambda slot: dstage.at[slot], lambda slot: drecv.at[slot], dsend, drsem, osem, credit,
    )
    weight_grad(hid, cot, gwo, True, False)

    def ng_step(k, carry):
        source = flip(r, k, n)

        @pl.when(k > 0)
        def _():
            arrival(PG, pg.at[rows(source)], source, "row")
            pg_copy(k).wait_send()

        scatter_col(NG, k, pg, lambda left, t: dot(left, wi[cols(t, wd), :], 1, 1), rng, dl)
        return carry

    lax.fori_loop(0, n, ng_step, 0)
    weight_grad(nrm, pg, gwi, False, True)

    for k in range(1, n):
        arrival(NG, rng.at[flip(c, k, n)], flip(c, k, n), "col")
    total = rng[0].astype(F32)
    for q in range(1, n):
        total = total + rng[q].astype(F32)
    centred = (patches[...].astype(F32) - average) * inverse
    weighted = total * centred
    ggr[c] = jnp.broadcast_to(jnp.sum(weighted, axis=0, keepdims=True), (8, dl))
    scaled = total * gain[...]
    st2[r] = jnp.where(
        lane == 0, jnp.sum(scaled, axis=1, keepdims=True),
        jnp.sum(weighted * gain[...], axis=1, keepdims=True),
    )
    for k in range(1, n):
        copy(ST2, st2.at[r], st2.at[r], k, r, "row", flip(r, k, n)).start()
        copy(GG, ggr.at[c], ggr.at[c], k, c, "col", flip(c, k, n)).start()
    for k in range(1, n):
        arrival(BR, rbr.at[flip(c, k, n)], flip(c, k, n), "col")
    out = rbr[0].astype(F32)
    for q in range(1, n):
        out = out + rbr[q].astype(F32)
    branch[...] = out.astype(BF16)

    for k in range(1, n):
        arrival(GG, ggr.at[flip(c, k, n)], flip(c, k, n), "col")
    own = ggr[0]
    for q in range(1, n):
        own = own + ggr[q]
    ggd[0] = own
    gain_copy = pltpu.make_async_remote_copy(
        src_ref=ggd.at[0], dst_ref=ggd.at[1], send_sem=ggsem.at[0], recv_sem=ggsem.at[1],
        device_id={"dp": 1 - d}, device_id_type=MESH,
    )
    gain_copy.start()
    for k in range(1, n):
        arrival(ST2, st2.at[flip(r, k, n)], flip(r, k, n), "row")
    sums = st2[0]
    for q in range(1, n):
        sums = sums + st2[q]
    first, second = sums[:, 0:1] / D, sums[:, 1:2] / D
    total = rng[0].astype(F32)
    for q in range(1, n):
        total = total + rng[q].astype(F32)
    centred = (patches[...].astype(F32) - average) * inverse
    grad_patches[...] = (inverse * (total * gain[...] - first - centred * second)).astype(BF16)
    gain_copy.wait()
    ggain[...] = ggd[0] + ggd[1]

    for k in range(1, n):
        copy(ST1, st1.at[r], st1.at[r], k, r, "row", flip(r, k, n)).wait_send()
        copy(ST2, st2.at[r], st2.at[r], k, r, "row", flip(r, k, n)).wait_send()
        copy(GG, ggr.at[c], ggr.at[c], k, c, "col", flip(c, k, n)).wait_send()
        br_copy(BR, rbr, flip(c, k, n), 0).wait_send()
        br_copy(NG, rng, flip(c, k, n), dl).wait_send()


def shards(n, patches, norm_gain, w_in, w_out, out_grad):
    tb, dl = patches.shape
    fl = w_in.shape[1]
    tm = 512 if dl % 512 == 0 and fl % 512 == 0 else 128
    tn = dl // 2 if dl % 256 == 0 else dl
    vmem = pl.BlockSpec(memory_space=pltpu.VMEM)
    hbm = pl.BlockSpec(memory_space=pl.ANY)
    out = jax.ShapeDtypeStruct
    flops = 12 * n * tb * dl * fl
    split = tb % (16 * n) == 0
    block = pltpu.VMEM((n, tb, fl), BF16)
    if split:
        body = kernel_split
        exchange = []
        landing = [pltpu.VMEM((n - 1, tb, fl), BF16)] * 2 + [block, pltpu.VMEM((n * tb, fl), BF16)] + [pltpu.VMEM((n - 1, tb, dl), BF16)] * 2
    else:
        body = kernel
        exchange = [pltpu.VMEM((2, tm, tn), BF16)] * 2
        landing = [block] * 3 + [pltpu.VMEM((n, tb, dl), BF16)] * 2
    branch, grad_patches, gwi, gwo, ggain = pl.pallas_call(
        functools.partial(body, n),
        out_shape=(
            out((tb, dl), BF16), out((tb, dl), BF16), out((dl, fl), BF16), out((fl, dl), BF16), out((8, dl), F32),
        ),
        in_specs=[vmem, vmem, hbm, hbm, hbm],
        out_specs=(vmem, vmem, hbm, hbm, vmem),
        scratch_shapes=[
            pltpu.VMEM((dl, fl), BF16),
            pltpu.VMEM((fl, dl), BF16),
            pltpu.VMEM((n * tb, dl), BF16),
            pltpu.VMEM((n * tb, dl), BF16),
            pltpu.VMEM((n * tb, fl), BF16),
            pltpu.VMEM((n * tb, fl), BF16),
            *landing,
            pltpu.VMEM((n, tb, 128), F32),
            pltpu.VMEM((n, tb, 128), F32),
            pltpu.VMEM((n, 8, dl), F32),
            pltpu.VMEM((2, 8, dl), F32),
            pltpu.VMEM((tm, n * tb), BF16),
            *exchange,
            pltpu.SemaphoreType.DMA((3,)),
            pltpu.SemaphoreType.DMA((11, n * n if split else n)),
            pltpu.SemaphoreType.DMA((11, n * n if split else n)),
            pltpu.SemaphoreType.DMA((2,)),
            pltpu.SemaphoreType.DMA((2,)),
            pltpu.SemaphoreType.DMA((2,)),
            pltpu.SemaphoreType.DMA((2,)),
            pltpu.SemaphoreType.REGULAR,
        ],
        compiler_params=pltpu.CompilerParams(
            collective_id=0, has_side_effects=True, vmem_limit_bytes=63 * 1024 * 1024
        ),
        cost_estimate=pl.CostEstimate(flops=flops, bytes_accessed=8 * dl * fl, transcendentals=tb * fl),
    )(patches, norm_gain.reshape(1, dl), w_in, w_out, out_grad)
    return branch, grad_patches, gwi.astype(F32), gwo.astype(F32), ggain[0]


def solution(mesh):
    n = mesh.shape["row"]
    if mesh.shape["col"] != n or mesh.shape["dp"] != 2 or n & (n - 1):
        raise ValueError("unsupported mesh")
    return jax.shard_map(
        functools.partial(shards, n),
        mesh=mesh,
        in_specs=(
            P(("dp", "col"), "row"),
            P("row"),
            P("row", "col"),
            P("col", "row"),
            P(("dp", "col"), "row"),
        ),
        out_specs=(
            P(("dp", "col"), "row"),
            P(("dp", "col"), "row"),
            P("row", "col"),
            P("col", "row"),
            P("row"),
        ),
        check_vma=False,
    )
```

```python
import functools

import jax
import jax.numpy as jnp
from jax import lax
from jax.experimental import pallas as pl
from jax.experimental.pallas import tpu as pltpu
from jax.sharding import PartitionSpec as P

D = 6144
MESH = pl.DeviceIdType.MESH
F32 = jnp.float32
BF16 = jnp.bfloat16

COT, NRM, HG, PRE, HID, PG, BR, NG, ST1, ST2, GG = range(11)


def flip(i, k, n):
    total, bit = 0, 1
    while bit < n:
        k_bit = (k // bit) % 2 if isinstance(k, int) else lax.rem(lax.div(k, jnp.int32(bit)), jnp.int32(2))
        i_bit = lax.rem(lax.div(i, jnp.int32(bit)), jnp.int32(2))
        total = total + lax.rem(i_bit + k_bit, jnp.int32(2)) * bit
        bit *= 2
    return total


def dot(left, right, left_dim=1, right_dim=0):
    return lax.dot_general(left, right, (((left_dim,), (right_dim,)), ((), ())), preferred_element_type=F32)


def gelu_and_slope(x):
    a, b = 0.7978845608028654, 0.044715
    square = x * x
    t = jnp.tanh(a * (x + b * (square * x)))
    half = 0.5 * (1.0 + t)
    return x * half, half + 0.5 * x * (1.0 - t * t) * (a * (1.0 + 3.0 * b * square))


def weight_grads(tile, wd, dl, d, lhs, dstage, drecv, dsend, drsem, osem, credit):
    def cols(t, width, start=0):
        return pl.ds(pl.multiple_of(start + t * width, width), width)

    def tile_copy(slot):
        return pltpu.make_async_remote_copy(
            src_ref=dstage.at[slot], dst_ref=drecv.at[slot], send_sem=dsend.at[slot], recv_sem=drsem.at[slot],
            device_id={"dp": 1 - d}, device_id_type=MESH,
        )

    def weight_grad(left, right, out, per_row, first, last):
        count = (out.shape[0] // tile) * per_row

        def place(t):
            if per_row == 1:
                return out.at[cols(t, tile), :]
            return out.at[cols(lax.div(t, jnp.int32(per_row)), tile), cols(lax.rem(t, jnp.int32(per_row)), dl)]

        def result_copy(t):
            slot = lax.rem(t, jnp.int32(2))
            return pltpu.make_async_copy(drecv.at[slot], place(t), osem.at[slot])

        def finish(t):
            slot = lax.rem(t, jnp.int32(2))
            tile_copy(slot).wait_send()
            tile_copy(slot).wait_recv()
            drecv[slot] = (dstage[slot].astype(F32) + drecv[slot].astype(F32)).astype(BF16)
            result_copy(t).start()

        def retire(t):
            result_copy(t).wait()

            def free():
                pl.semaphore_signal(credit, inc=1, device_id={"dp": 1 - d}, device_id_type=MESH)

            if last:
                pl.when(t < count - 2)(free)
            else:
                free()

        def step(t, carry):
            slot = lax.rem(t, jnp.int32(2))
            lhs[...] = left[:, cols(lax.div(t, jnp.int32(per_row)), tile)].T
            shift = lax.rem(t, jnp.int32(per_row)) * dl

            def part(p, inner):
                dstage[slot, :, cols(p, wd)] = dot(
                    lhs[...], right[:, pl.ds(pl.multiple_of(shift + p * wd, wd), wd)]
                ).astype(BF16)
                return inner

            lax.fori_loop(0, dl // wd, part, 0)

            @pl.when(t >= 2)
            def _():
                retire(t - 2)

            def claim():
                pl.semaphore_wait(credit, 1)

            if first:
                pl.when(t >= 2)(claim)
            else:
                claim()
            tile_copy(slot).start()

            @pl.when(t >= 1)
            def _():
                finish(t - 1)

            return carry

        lax.fori_loop(0, count, step, 0)
        finish(jnp.int32(count - 1))
        retire(jnp.int32(count - 2))
        retire(jnp.int32(count - 1))

    return weight_grad


def kernel_split(
    n, patches, gain, w_in, w_out, out_grad,
    branch, grad_patches, gwi, gwo, ggain,
    wi, wo, cot, nrm, hid, pg, rhg, rpre, stage, stage2, rbr, rng, st1, st2, ggr, ggd, lhs, dstage, drecv,
    wsem, send, recv, dsend, drsem, osem, ggsem, credit,
):
    tb, dl = patches.shape
    fl = w_in.shape[1]
    sb = tb // n
    wf = 256 if fl % 256 == 0 else 128
    wd = 256 if dl % 256 == 0 else 128
    tile = dstage.shape[1]
    r, c, d = lax.axis_index("row"), lax.axis_index("col"), lax.axis_index("dp")
    weight_grad = weight_grads(tile, wd, dl, d, lhs, dstage, drecv, dsend, drsem, osem, credit)

    def rows(j):
        return pl.ds(pl.multiple_of(j * tb, tb), tb)

    def piece(j, q):
        return pl.ds(pl.multiple_of(j * tb + q * sb, sb), sb)

    def part(q):
        return pl.ds(pl.multiple_of(q * sb, sb), sb)

    def cols(t, width, start=0):
        return pl.ds(pl.multiple_of(start + t * width, width), width)

    load_out = pltpu.make_async_copy(w_out, wo, wsem.at[0])
    load_in = pltpu.make_async_copy(w_in, wi, wsem.at[1])
    load_out.start()
    load_in.start()

    barrier = pltpu.get_barrier_semaphore()
    for k in range(1, n):
        pl.semaphore_signal(barrier, inc=1, device_id={"row": flip(r, k, n)}, device_id_type=MESH)
        pl.semaphore_signal(barrier, inc=1, device_id={"col": flip(c, k, n)}, device_id_type=MESH)
    pl.semaphore_signal(barrier, inc=1, device_id={"dp": 1 - d}, device_id_type=MESH)
    pl.semaphore_wait(barrier, 2 * (n - 1) + 1)

    def copy(kind, src, dst, at, axis, peer):
        return pltpu.make_async_remote_copy(
            src_ref=src, dst_ref=dst, send_sem=send.at[kind, at], recv_sem=recv.at[kind, at],
            device_id={axis: peer}, device_id_type=MESH,
        )

    def cot_copy(k):
        return copy(COT, out_grad, cot.at[rows(c)], k, "col", flip(c, k, n))

    def nrm_copy(k):
        return copy(NRM, nrm.at[rows(c)], nrm.at[rows(c)], k, "col", flip(c, k, n))

    def st1_copy(m):
        return copy(ST1, st1.at[0], st1.at[m], m, "row", flip(r, m, n))

    def st2_copy(m):
        return copy(ST2, st2.at[0], st2.at[m], m, "row", flip(r, m, n))

    def gg_copy(k):
        return copy(GG, ggr.at[0], ggr.at[k], k, "col", flip(c, k, n))

    def scatter_copy(kind, src, dst, j, m):
        peer = flip(r, m, n)
        return copy(kind, src.at[j, part(peer)], dst.at[m - 1, part(j)], j * n + m, "row", peer)

    def gather_copy(kind, panel, j, m):
        return copy(kind, panel.at[piece(j, r)], panel.at[piece(j, r)], j * n + m, "row", flip(r, m, n))

    def back_copy(kind, dst, k, start):
        j = flip(c, k, n)
        return copy(kind, stage.at[j, :, pl.ds(start, dl)], dst.at[k - 1], k, "col", j)

    cot_copy(1).start()
    if n > 2:
        cot_copy(2).start()
    own_cot = pltpu.make_async_copy(out_grad, cot.at[rows(c)], wsem.at[2])
    own_cot.start()

    values = patches[...].astype(F32)
    lane = lax.broadcasted_iota(jnp.int32, (tb, 128), 1)
    st1[0] = jnp.where(
        lane == 0, jnp.sum(values, axis=1, keepdims=True), jnp.sum(values * values, axis=1, keepdims=True)
    )
    for m in range(1, n):
        st1_copy(m).start()

    def hid_grad_terms(j):
        def body(t, carry):
            stage[j, :, cols(t, wf)] = dot(cot[rows(j), :], wo[cols(t, wf), :], 1, 1).astype(BF16)
            return carry

        lax.fori_loop(0, fl // wf, body, 0)
        for m in range(1, n):
            scatter_copy(HG, stage, rhg, j, m).start()

    def pre_terms(j):
        def body(t, carry):
            stage2[j, :, cols(t, wf)] = dot(nrm[rows(j), :], wi[:, cols(t, wf)]).astype(BF16)
            return carry

        lax.fori_loop(0, fl // wf, body, 0)
        for m in range(1, n):
            scatter_copy(PRE, stage2, rpre, j, m).start()

    def hidden(j):
        for m in range(1, n):
            scatter_copy(HG, stage, rhg, j, m).wait_recv()
            scatter_copy(PRE, stage2, rpre, j, m).wait_recv()

        def body(t, carry):
            at = cols(t, wf)
            pre, grad = stage2[j, part(r), at].astype(F32), stage[j, part(r), at].astype(F32)
            for m in range(1, n):
                pre = pre + rpre[m - 1, part(j), at].astype(F32)
                grad = grad + rhg[m - 1, part(j), at].astype(F32)
            activation, slope = gelu_and_slope(pre)
            hid[piece(j, r), at] = activation.astype(BF16)
            pg[piece(j, r), at] = (grad * slope).astype(BF16)
            return carry

        lax.fori_loop(0, fl // wf, body, 0)
        for m in range(1, n):
            gather_copy(HID, hid, j, m).start()
        for m in range(1, n):
            gather_copy(PG, pg, j, m).start()

    def back(k):
        j = flip(c, k, n)
        for m in range(1, n):
            scatter_copy(HG, stage, rhg, j, m).wait_send()
        for m in range(1, n):
            gather_copy(HID, hid, j, m).wait_recv()

        def branch_body(t, carry):
            stage[j, :, cols(t, wd)] = dot(hid[rows(j), :], wo[:, cols(t, wd)]).astype(BF16)
            return carry

        lax.fori_loop(0, dl // wd, branch_body, 0)
        if k > 0:
            back_copy(BR, rbr, k, 0).start()
        for m in range(1, n):
            gather_copy(PG, pg, j, m).wait_recv()

        def grad_body(t, carry):
            stage[j, :, cols(t, wd, dl)] = dot(pg[rows(j), :], wi[cols(t, wd), :], 1, 1).astype(BF16)
            return carry

        lax.fori_loop(0, dl // wd, grad_body, 0)
        if k > 0:
            back_copy(NG, rng, k, dl).start()

    own_cot.wait()
    load_out.wait()
    hid_grad_terms(c)

    sums = st1[0]
    for m in range(1, n):
        st1_copy(m).wait_recv()
        sums = sums + st1[m]
    average = sums[:, 0:1] / D
    inverse = lax.rsqrt(sums[:, 1:2] / D - average * average + 1e-06)
    nrm[rows(c), :] = ((patches[...].astype(F32) - average) * inverse * gain[...]).astype(BF16)
    nrm_copy(1).start()
    if n > 2:
        nrm_copy(2).start()
    load_in.wait()
    pre_terms(c)

    for k in range(1, n):
        cot_copy(k).wait_recv()
        if k + 2 < n:
            cot_copy(k).wait_send()
            cot_copy(k + 2).start()
        hid_grad_terms(flip(c, k, n))
        nrm_copy(k).wait_recv()
        if k + 2 < n:
            nrm_copy(k).wait_send()
            nrm_copy(k + 2).start()
        pre_terms(flip(c, k, n))
        hidden(flip(c, k - 1, n))
        if k > 1:
            back(k - 2)
    hidden(flip(c, n - 1, n))
    for k in range(max(n - 2, 0), n):
        back(k)

    weight_grad(hid, cot, gwo, 1, True, False)
    weight_grad(nrm, pg, gwi, fl // dl, False, True)

    def sum_back(dst, start):
        total = stage[c, :, pl.ds(start, dl)].astype(F32)
        for k in range(1, n):
            total = total + dst[k - 1].astype(F32)
        return total

    for k in range(1, n):
        back_copy(NG, rng, k, dl).wait_recv()
    total = sum_back(rng, dl)
    weighted = total * ((patches[...].astype(F32) - average) * inverse)
    ggr[0] = jnp.broadcast_to(jnp.sum(weighted, axis=0, keepdims=True), (8, dl))
    st2[0] = jnp.where(
        lane == 0, jnp.sum(total * gain[...], axis=1, keepdims=True),
        jnp.sum(weighted * gain[...], axis=1, keepdims=True),
    )
    for m in range(1, n):
        st2_copy(m).start()
    for k in range(1, n):
        gg_copy(k).start()
    for k in range(1, n):
        back_copy(BR, rbr, k, 0).wait_recv()
    branch[...] = sum_back(rbr, 0).astype(BF16)
    own = ggr[0]
    for k in range(1, n):
        gg_copy(k).wait_recv()
        own = own + ggr[k]
    ggd[0] = own
    gain_copy = pltpu.make_async_remote_copy(
        src_ref=ggd.at[0], dst_ref=ggd.at[1], send_sem=ggsem.at[0], recv_sem=ggsem.at[1],
        device_id={"dp": 1 - d}, device_id_type=MESH,
    )
    gain_copy.start()

    sums = st2[0]
    for m in range(1, n):
        st2_copy(m).wait_recv()
        sums = sums + st2[m]
    first, second = sums[:, 0:1] / D, sums[:, 1:2] / D
    centred = (patches[...].astype(F32) - average) * inverse
    grad_patches[...] = (inverse * (sum_back(rng, dl) * gain[...] - first - centred * second)).astype(BF16)
    gain_copy.wait()
    ggain[...] = ggd[0] + ggd[1]

    for m in range(1, n):
        st1_copy(m).wait_send()
        st2_copy(m).wait_send()
        gg_copy(m).wait_send()
        back_copy(BR, rbr, m, 0).wait_send()
        back_copy(NG, rng, m, dl).wait_send()
        if m + 2 >= n:
            cot_copy(m).wait_send()
            nrm_copy(m).wait_send()
        for k in range(n):
            j = flip(c, k, n)
            scatter_copy(PRE, stage2, rpre, j, m).wait_send()
            gather_copy(HID, hid, j, m).wait_send()
            gather_copy(PG, pg, j, m).wait_send()


def kernel(
    n, patches, gain, w_in, w_out, out_grad,
    branch, grad_patches, gwi, gwo, ggain,
    wi, wo, cot, nrm, hid, pg, rhg, rpre, stage, rbr, rng, st1, st2, ggr, ggd, lhs, dstage, drecv,
    wsem, send, recv, dsend, drsem, osem, ggsem, credit,
):
    tb, dl = patches.shape
    fl = w_in.shape[1]
    wf = 256 if fl % 256 == 0 else 128
    wd = 256 if dl % 256 == 0 else 128
    tile = dstage.shape[1]
    r, c, d = lax.axis_index("row"), lax.axis_index("col"), lax.axis_index("dp")

    def rows(j):
        return pl.ds(pl.multiple_of(j * tb, tb), tb)

    def cols(t, width, start=0):
        return pl.ds(pl.multiple_of(start + t * width, width), width)

    load_out = pltpu.make_async_copy(w_out, wo, wsem.at[0])
    load_in = pltpu.make_async_copy(w_in, wi, wsem.at[1])
    load_out.start()
    load_in.start()

    barrier = pltpu.get_barrier_semaphore()
    for k in range(1, n):
        pl.semaphore_signal(barrier, inc=1, device_id={"row": flip(r, k, n)}, device_id_type=MESH)
        pl.semaphore_signal(barrier, inc=1, device_id={"col": flip(c, k, n)}, device_id_type=MESH)
    pl.semaphore_signal(barrier, inc=1, device_id={"dp": 1 - d}, device_id_type=MESH)
    pl.semaphore_wait(barrier, 2 * (n - 1) + 1)

    def copy(kind, src, dst, send_at, recv_at, axis, peer):
        return pltpu.make_async_remote_copy(
            src_ref=src, dst_ref=dst, send_sem=send.at[kind, send_at], recv_sem=recv.at[kind, recv_at],
            device_id={axis: peer}, device_id_type=MESH,
        )

    def cot_copy(k):
        return copy(COT, out_grad, cot.at[rows(c)], k, c, "col", flip(c, k, n))

    def nrm_copy(k):
        return copy(NRM, nrm.at[rows(c)], nrm.at[rows(c)], k, c, "col", flip(c, k, n))

    def hid_copy(k):
        return copy(HID, hid.at[rows(r)], hid.at[rows(r)], k, r, "row", flip(r, k, n))

    def pg_copy(k):
        return copy(PG, pg.at[rows(r)], pg.at[rows(r)], k, r, "row", flip(r, k, n))

    def arrival(kind, ref, source, axis):
        copy(kind, ref, ref, 0, source, axis, source).wait_recv()

    for k in range(1, n):
        cot_copy(k).start()
    own_cot = pltpu.make_async_copy(out_grad, cot.at[rows(c)], wsem.at[2])
    own_cot.start()

    values = patches[...].astype(F32)
    lane = lax.broadcasted_iota(jnp.int32, (tb, 128), 1)
    st1[r] = jnp.where(
        lane == 0, jnp.sum(values, axis=1, keepdims=True), jnp.sum(values * values, axis=1, keepdims=True)
    )
    for k in range(1, n):
        copy(ST1, st1.at[r], st1.at[r], k, r, "row", flip(r, k, n)).start()

    def hg_copy(kind, dst, j):
        return copy(kind, stage.at[j], dst.at[r], j, r, "row", j)

    def scatter_row(kind, k, panel, product, dst):
        j = flip(c, k, n)
        mine = j == r

        if kind == PRE:
            @pl.when(jnp.logical_not(mine))
            def _():
                hg_copy(HG, rhg, j).wait_send()

        def body(t, carry):
            term = product(panel[rows(j), :], t).astype(BF16)

            @pl.when(mine)
            def _():
                dst[r, :, cols(t, wf)] = term

            @pl.when(jnp.logical_not(mine))
            def _():
                stage[j, :, cols(t, wf)] = term

            return carry

        lax.fori_loop(0, fl // wf, body, 0)

        @pl.when(jnp.logical_not(mine))
        def _():
            hg_copy(kind, dst, j).start()

    def hg_product(left, t):
        return dot(left, wo[cols(t, wf), :], 1, 1)

    def pre_product(left, t):
        return dot(left, wi[:, cols(t, wf)])

    own_cot.wait()
    load_out.wait()
    scatter_row(HG, jnp.int32(0), cot, hg_product, rhg)

    for k in range(1, n):
        arrival(ST1, st1.at[flip(r, k, n)], flip(r, k, n), "row")
    sums = st1[0]
    for q in range(1, n):
        sums = sums + st1[q]
    average = sums[:, 0:1] / D
    inverse = lax.rsqrt(sums[:, 1:2] / D - average * average + 1e-06)
    nrm[rows(c), :] = ((patches[...].astype(F32) - average) * inverse * gain[...]).astype(BF16)

    def hg_step(k, carry):
        source = flip(c, k, n)
        arrival(COT, cot.at[rows(source)], source, "col")
        cot_copy(k).wait_send()
        nrm_copy(k).start()
        scatter_row(HG, k, cot, hg_product, rhg)
        return carry

    lax.fori_loop(1, n, hg_step, 0)
    load_in.wait()

    def pre_step(k, carry):
        source = flip(c, k, n)

        @pl.when(k > 0)
        def _():
            arrival(NRM, nrm.at[rows(source)], source, "col")
            nrm_copy(k).wait_send()

        scatter_row(PRE, k, nrm, pre_product, rpre)
        return carry

    lax.fori_loop(0, n, pre_step, 0)

    for k in range(1, n):
        source = flip(r, k, n)
        arrival(HG, rhg.at[source], source, "row")
        arrival(PRE, rpre.at[source], source, "row")

    def hidden_step(t, carry):
        at = cols(t, wf)
        pre, grad = rpre[0, :, at].astype(F32), rhg[0, :, at].astype(F32)
        for q in range(1, n):
            pre = pre + rpre[q, :, at].astype(F32)
            grad = grad + rhg[q, :, at].astype(F32)
        activation, slope = gelu_and_slope(pre)
        hid[rows(r), at] = activation.astype(BF16)
        pg[rows(r), at] = (grad * slope).astype(BF16)
        return carry

    lax.fori_loop(0, fl // wf, hidden_step, 0)
    for k in range(1, n):
        hid_copy(k).start()
    for k in range(1, n):
        hg_copy(PRE, rpre, flip(r, k, n)).wait_send()

    def br_copy(kind, dst, j, start):
        return copy(kind, stage.at[j, :, pl.ds(start, dl)], dst.at[c], j, c, "col", j)

    def scatter_col(kind, k, panel, product, dst, start):
        j = flip(r, k, n)
        mine = j == c

        def body(t, carry):
            term = product(panel[rows(j), :], t).astype(BF16)

            @pl.when(mine)
            def _():
                dst[c, :, cols(t, wd)] = term

            @pl.when(jnp.logical_not(mine))
            def _():
                stage[j, :, cols(t, wd, start)] = term

            return carry

        lax.fori_loop(0, dl // wd, body, 0)

        @pl.when(jnp.logical_not(mine))
        def _():
            br_copy(kind, dst, j, start).start()

    def branch_step(k, carry):
        source = flip(r, k, n)

        @pl.when(k > 0)
        def _():
            arrival(HID, hid.at[rows(source)], source, "row")
            hid_copy(k).wait_send()
            pg_copy(k).start()

        scatter_col(BR, k, hid, lambda left, t: dot(left, wo[:, cols(t, wd)]), rbr, 0)
        return carry

    lax.fori_loop(0, n, branch_step, 0)

    weight_grad = weight_grads(tile, wd, dl, d, lhs, dstage, drecv, dsend, drsem, osem, credit)
    weight_grad(hid, cot, gwo, 1, True, False)

    def ng_step(k, carry):
        source = flip(r, k, n)

        @pl.when(k > 0)
        def _():
            arrival(PG, pg.at[rows(source)], source, "row")
            pg_copy(k).wait_send()

        scatter_col(NG, k, pg, lambda left, t: dot(left, wi[cols(t, wd), :], 1, 1), rng, dl)
        return carry

    lax.fori_loop(0, n, ng_step, 0)
    weight_grad(nrm, pg, gwi, fl // dl, False, True)

    for k in range(1, n):
        arrival(NG, rng.at[flip(c, k, n)], flip(c, k, n), "col")
    total = rng[0].astype(F32)
    for q in range(1, n):
        total = total + rng[q].astype(F32)
    centred = (patches[...].astype(F32) - average) * inverse
    weighted = total * centred
    ggr[c] = jnp.broadcast_to(jnp.sum(weighted, axis=0, keepdims=True), (8, dl))
    scaled = total * gain[...]
    st2[r] = jnp.where(
        lane == 0, jnp.sum(scaled, axis=1, keepdims=True),
        jnp.sum(weighted * gain[...], axis=1, keepdims=True),
    )
    for k in range(1, n):
        copy(ST2, st2.at[r], st2.at[r], k, r, "row", flip(r, k, n)).start()
        copy(GG, ggr.at[c], ggr.at[c], k, c, "col", flip(c, k, n)).start()
    for k in range(1, n):
        arrival(BR, rbr.at[flip(c, k, n)], flip(c, k, n), "col")
    out = rbr[0].astype(F32)
    for q in range(1, n):
        out = out + rbr[q].astype(F32)
    branch[...] = out.astype(BF16)

    for k in range(1, n):
        arrival(GG, ggr.at[flip(c, k, n)], flip(c, k, n), "col")
    own = ggr[0]
    for q in range(1, n):
        own = own + ggr[q]
    ggd[0] = own
    gain_copy = pltpu.make_async_remote_copy(
        src_ref=ggd.at[0], dst_ref=ggd.at[1], send_sem=ggsem.at[0], recv_sem=ggsem.at[1],
        device_id={"dp": 1 - d}, device_id_type=MESH,
    )
    gain_copy.start()
    for k in range(1, n):
        arrival(ST2, st2.at[flip(r, k, n)], flip(r, k, n), "row")
    sums = st2[0]
    for q in range(1, n):
        sums = sums + st2[q]
    first, second = sums[:, 0:1] / D, sums[:, 1:2] / D
    total = rng[0].astype(F32)
    for q in range(1, n):
        total = total + rng[q].astype(F32)
    centred = (patches[...].astype(F32) - average) * inverse
    grad_patches[...] = (inverse * (total * gain[...] - first - centred * second)).astype(BF16)
    gain_copy.wait()
    ggain[...] = ggd[0] + ggd[1]

    for k in range(1, n):
        copy(ST1, st1.at[r], st1.at[r], k, r, "row", flip(r, k, n)).wait_send()
        copy(ST2, st2.at[r], st2.at[r], k, r, "row", flip(r, k, n)).wait_send()
        copy(GG, ggr.at[c], ggr.at[c], k, c, "col", flip(c, k, n)).wait_send()
        br_copy(BR, rbr, flip(c, k, n), 0).wait_send()
        br_copy(NG, rng, flip(c, k, n), dl).wait_send()


def shards(n, patches, norm_gain, w_in, w_out, out_grad):
    tb, dl = patches.shape
    fl = w_in.shape[1]
    tile = 256 if dl % 256 == 0 and fl % 256 == 0 else 128
    vmem = pl.BlockSpec(memory_space=pltpu.VMEM)
    hbm = pl.BlockSpec(memory_space=pl.ANY)
    out = jax.ShapeDtypeStruct
    flops = 12 * n * tb * dl * fl
    split = tb % (16 * n) == 0
    block = pltpu.VMEM((n, tb, fl), BF16)
    if split:
        body = kernel_split
        landing = [pltpu.VMEM((n - 1, tb, fl), BF16)] * 2 + [block] * 2 + [pltpu.VMEM((n - 1, tb, dl), BF16)] * 2
    else:
        body = kernel
        landing = [block] * 3 + [pltpu.VMEM((n, tb, dl), BF16)] * 2
    branch, grad_patches, gwi, gwo, ggain = pl.pallas_call(
        functools.partial(body, n),
        out_shape=(
            out((tb, dl), BF16), out((tb, dl), BF16), out((dl, fl), BF16), out((fl, dl), BF16), out((8, dl), F32),
        ),
        in_specs=[vmem, vmem, hbm, hbm, hbm],
        out_specs=(vmem, vmem, hbm, hbm, vmem),
        scratch_shapes=[
            pltpu.VMEM((dl, fl), BF16),
            pltpu.VMEM((fl, dl), BF16),
            pltpu.VMEM((n * tb, dl), BF16),
            pltpu.VMEM((n * tb, dl), BF16),
            pltpu.VMEM((n * tb, fl), BF16),
            pltpu.VMEM((n * tb, fl), BF16),
            *landing,
            pltpu.VMEM((n, tb, 128), F32),
            pltpu.VMEM((n, tb, 128), F32),
            pltpu.VMEM((n, 8, dl), F32),
            pltpu.VMEM((2, 8, dl), F32),
            pltpu.VMEM((tile, n * tb), BF16),
            pltpu.VMEM((2, tile, dl), BF16),
            pltpu.VMEM((2, tile, dl), BF16),
            pltpu.SemaphoreType.DMA((3,)),
            pltpu.SemaphoreType.DMA((11, n * n if split else n)),
            pltpu.SemaphoreType.DMA((11, n * n if split else n)),
            pltpu.SemaphoreType.DMA((2,)),
            pltpu.SemaphoreType.DMA((2,)),
            pltpu.SemaphoreType.DMA((2,)),
            pltpu.SemaphoreType.DMA((2,)),
            pltpu.SemaphoreType.REGULAR,
        ],
        compiler_params=pltpu.CompilerParams(
            collective_id=0, has_side_effects=True, vmem_limit_bytes=63 * 1024 * 1024
        ),
        cost_estimate=pl.CostEstimate(flops=flops, bytes_accessed=8 * dl * fl, transcendentals=tb * fl),
    )(patches, norm_gain.reshape(1, dl), w_in, w_out, out_grad)
    return branch, grad_patches, gwi.astype(F32), gwo.astype(F32), ggain[0]


def solution(mesh):
    n = mesh.shape["row"]
    if mesh.shape["col"] != n or mesh.shape["dp"] != 2 or n & (n - 1):
        raise ValueError("unsupported mesh")
    return jax.shard_map(
        functools.partial(shards, n),
        mesh=mesh,
        in_specs=(
            P(("dp", "col"), "row"),
            P("row"),
            P("row", "col"),
            P("col", "row"),
            P(("dp", "col"), "row"),
        ),
        out_specs=(
            P(("dp", "col"), "row"),
            P(("dp", "col"), "row"),
            P("row", "col"),
            P("col", "row"),
            P("row"),
        ),
        check_vma=False,
    )
```
